256 devices in a mesh: depth: 8 (over z), rows: 32 (over x, y, core).
Axes of the slice: x: 4, y: 4, z: 8, core: 2. Of those that a mesh axis runs over, the one named last changes fastest.
Arguments:
- grad_arriving: float32 [8, 2, 2048, 2048], P('depth', None, 'rows'), may hold values from -6 to 6
- loss_grad: float32 [2, 2048, 2048], P(None, 'rows'), may hold values from -6 to 6
- t_entry: float32 [8, 2, 2048, 2048], P('depth', None, 'rows'), may hold values from -6 to 6
- t_exit: float32 [8, 2, 2048, 2048], P('depth', None, 'rows'), may hold values from -6 to 6
- fields_entry: float32 [8, 2, 2048, 2048], P('depth', None, 'rows'), may hold values from -6 to 6
- fields_exit: float32 [8, 2, 2048, 2048], P('depth', None, 'rows'), may hold values from -6 to 6
- led_index: int32 [8, 2], P('depth'), may hold values from 0 to 224
Outputs:
- grad_entry: float32 [8, 2, 2048, 2048], P('depth', None, 'rows')
- grad_exit: float32 [8, 2, 2048, 2048], P('depth', None, 'rows')
- leaving: float32 [8, 2, 2048, 2048], P('depth', None, 'rows')
The draws below stay inside these ranges and needn't reach their ends.
All inputs are finite; a program needn't handle non-finite values.
Results may differ from the reference program's by a relative error of at most 0.0001.
Values sent between devices are 32-bit elements; how exact they have to be, the bound alone decides.
No kernel may reach another device: no remote copies, remote signals or barrier semaphores. Data moves between devices by JAX's collectives and lax.ppermute only.
A program may use at most 128 MiB of HBM per device.

```python
import math
import jax
import jax.numpy as jnp

N = 2048
LED_SIDE = 15
N_DEPTH = 8


def with_ends(result, rng, smallest, top_value):
    longest = result.shape.index(max(result.shape))
    spots = []
    for shift in (0, 1):
        where = [jax.random.randint(jax.random.fold_in(rng, axis), (), 0, length) for axis, length in enumerate(result.shape)]
        where[longest] = (where[longest] + shift) % result.shape[longest]
        spots.append(tuple(where))
    return result.at[spots[0]].set(smallest).at[spots[1]].set(top_value)


def block_scale(rng, shape, cuts, least, largest):
    gain, own = 1.0, jax.random.fold_in(rng, 6)
    for position, blocks in cuts:
        steps = jnp.exp(jax.random.uniform(jax.random.fold_in(own, position), (blocks,), jnp.float32, least / len(cuts), largest / len(cuts)))
        gain = gain * jnp.repeat(steps, shape[position] // blocks).reshape([-1 if axis == position else 1 for axis in range(len(shape))])
    return gain


def normal_values(stream_key, extent, spread, limit, cuts=(), kind=jnp.bfloat16):
    entries = spread * jax.random.normal(stream_key, extent, jnp.float32)
    if cuts:
        entries = entries * block_scale(stream_key, extent, cuts, -0.22, 0.18)
    return jnp.clip(entries, -limit, limit).astype(kind)


def setup_inputs(seed: int = 0) -> dict:
    key_of = jax.random.split(jax.random.key(seed), 8)
    grad_arriving = normal_values(key_of[0], (N_DEPTH, 2, N, N), 1.0, 6.0, ((0, 8), (2, 32)), jnp.float32)
    loss_grad = normal_values(key_of[1], (2, N, N), 1.0, 6.0, ((1, 32),), jnp.float32)
    t_entry = normal_values(key_of[2], (N_DEPTH, 2, N, N), 1.0, 6.0, ((0, 8), (2, 32)), jnp.float32)
    t_exit = normal_values(key_of[3], (N_DEPTH, 2, N, N), 1.0, 6.0, ((0, 8), (2, 32)), jnp.float32)
    fields_entry = normal_values(key_of[4], (N_DEPTH, 2, N, N), 1.0, 6.0, ((0, 8), (2, 32)), jnp.float32)
    fields_exit = normal_values(key_of[5], (N_DEPTH, 2, N, N), 1.0, 6.0, ((0, 8), (2, 32)), jnp.float32)
    led_index = with_ends(jax.random.randint(key_of[6], (N_DEPTH, 2), 0, LED_SIDE * LED_SIDE), jax.random.fold_in(key_of[6], 1), 0, (LED_SIDE * LED_SIDE) - 1).astype(jnp.int32)
    return dict(grad_arriving=grad_arriving, loss_grad=loss_grad, t_entry=t_entry, t_exit=t_exit, fields_entry=fields_entry, fields_exit=fields_exit, led_index=led_index)


def make_complex(stacked):
    return stacked[0] + 1j * stacked[1]


def split_complex(values):
    return jnp.stack([jnp.real(values), jnp.imag(values)]).astype(jnp.float32)


def backward_kernel(length):
    idx_all = jnp.arange(length, dtype=jnp.int32)
    frequency = jnp.where(idx_all < length // 2, idx_all, idx_all - length)
    quad_phase = (3 * (frequency[:, None] * frequency[:, None] + frequency[None, :] * frequency[None, :])) % length
    phase_angle = (-2.0 * math.pi / length) * quad_phase.astype(jnp.float32)
    return jnp.exp(1j * phase_angle)


def illumination(length, led_number):
    shift_col = led_number // LED_SIDE - LED_SIDE // 2
    shift_row = led_number % LED_SIDE - LED_SIDE // 2
    row_ids = jnp.arange(length, dtype=jnp.int32)[:, None]
    col_ids = jnp.arange(length, dtype=jnp.int32)[None, :]
    quad_phase = (shift_col * col_ids + shift_row * row_ids) % length
    phase_angle = (2.0 * math.pi / length) * quad_phase.astype(jnp.float32)
    return jnp.exp(1j * phase_angle)


def backward_map(values, kernel):
    return jnp.fft.ifft2(kernel * jnp.fft.fft2(values))


def reference(grad_arriving, loss_grad, t_entry, t_exit, fields_entry, fields_exit, led_index):
    kernel = backward_kernel(N)
    entry_grads = []
    passing = []
    for section in range(N_DEPTH):
        wave = backward_map(make_complex(grad_arriving[section]), kernel)
        lit = make_complex(fields_entry[section]) * illumination(N, led_index[section, 0])
        entry_grads.append(split_complex(wave * jnp.conj(lit)))
        passing.append(wave * jnp.conj(make_complex(t_entry[section])))
    exit_grads = []
    leaving = []
    for section in range(N_DEPTH):
        if section == N_DEPTH - 1:
            second_input = make_complex(loss_grad)
        else:
            second_input = passing[section + 1]
        wave = backward_map(second_input, kernel)
        lit = make_complex(fields_exit[section]) * illumination(N, led_index[section, 1])
        exit_grads.append(split_complex(wave * jnp.conj(lit)))
        leaving.append(split_complex(wave * jnp.conj(make_complex(t_exit[section]))))
    return jnp.stack(entry_grads), jnp.stack(exit_grads), jnp.stack(leaving)
```

```python
import functools
import math

import jax
import jax.numpy as jnp
import numpy as np
from jax import lax
from jax.experimental import pallas as pl
from jax.experimental.pallas import tpu as pltpu
from jax.sharding import PartitionSpec as P

LED_SIDE = 15
SPREAD = 3
BLOCKS = 32
N = 2048
WIDTH = N // BLOCKS
LANES = 2 * WIDTH
CLASSES = 1
VMEM_LIMIT = 24 * 1024 * 1024

INVERSE = pow(SPREAD, -1, N)
_k = np.arange(N, dtype=np.int64)
GAUSS = np.exp(-2j * np.pi * ((SPREAD * _k * _k) % N) / N).sum() / N


def chirp_gain(distance):
    return complex(GAUSS * np.exp(2j * np.pi * ((INVERSE * distance * distance) % N) / N))


def shift_of(freq):
    return SPREAD * (freq - BLOCKS // 2) % BLOCKS


def lane_tables():
    own = np.zeros((BLOCKS, LANES), np.float32)
    other = np.zeros((BLOCKS, LANES), np.float32)
    for freq in range(BLOCKS):
        shift = shift_of(freq)
        plain = chirp_gain(-shift)
        wrapped = chirp_gain(BLOCKS - shift)
        for lane in range(LANES):
            sign = -1.0 if lane < WIDTH else 1.0
            if lane % WIDTH >= 2 * shift:
                own[freq, lane] = plain.real
                other[freq, lane] = plain.imag * sign
            else:
                own[freq, lane] = wrapped.imag * sign
                other[freq, lane] = wrapped.real
    return own, other


def lane_ids():
    return lax.broadcasted_iota(jnp.int32, (8, LANES), 1)


def times_i(value):
    sign = jnp.where(lane_ids() < WIDTH, -1.0, 1.0).astype(jnp.float32)
    return pltpu.roll(value, WIDTH, 1) * sign


def scaled(value, factor):
    return value * np.float32(factor.real) + times_i(value) * np.float32(factor.imag)


def turned(value, step, count, sign):
    step %= count
    if step == 0:
        return value
    if 4 * step == count:
        return times_i(value) if sign > 0 else -times_i(value)
    angle = 2.0 * math.pi * sign * step / count
    return scaled(value, complex(math.cos(angle), math.sin(angle)))


def small_dft(values, sign):
    count = len(values)
    if count == 1:
        return values
    if count == 2:
        return [values[0] + values[1], values[0] - values[1]]
    quarter = count // 4
    parts = [small_dft(values[phase::4], sign) for phase in range(4)]
    result = [None] * count
    for j in range(quarter):
        a = parts[0][j]
        b = turned(parts[1][j], j, count, sign)
        c = turned(parts[2][j], 2 * j, count, sign)
        d = turned(parts[3][j], 3 * j, count, sign)
        sum_ac, dif_ac, sum_bd = a + c, a - c, b + d
        dif_bd = times_i(b - d)
        result[j] = sum_ac + sum_bd
        result[j + 2 * quarter] = sum_ac - sum_bd
        if sign > 0:
            result[j + quarter] = dif_ac + dif_bd
            result[j + 3 * quarter] = dif_ac - dif_bd
        else:
            result[j + quarter] = dif_ac - dif_bd
            result[j + 3 * quarter] = dif_ac + dif_bd
    return result


def pack(real, imag):
    low = lane_ids() < WIDTH
    return (
        jnp.where(low, real, pltpu.roll(imag, WIDTH, 1)),
        jnp.where(low, pltpu.roll(real, WIDTH, 1), imag),
    )


def unpack(first, second):
    low = lane_ids() < WIDTH
    return (
        jnp.where(low, first, pltpu.roll(second, WIDTH, 1)),
        jnp.where(low, pltpu.roll(first, WIDTH, 1), second),
    )


def along_lanes(blocks, own_ref, other_ref):
    spectrum = small_dft(blocks, -1)
    moved = []
    for freq, value in enumerate(spectrum):
        shift = 2 * shift_of(freq)
        straight = pltpu.roll(value, shift, 1) if shift else value
        crossed = pltpu.roll(value, shift + WIDTH, 1)
        moved.append(
            straight * own_ref[freq : freq + 1, :] + crossed * other_ref[freq : freq + 1, :]
        )
    return small_dft(moved, 1)


def rows_at(group):
    return pl.ds(pl.multiple_of(group * 8, 8), 8)


def natural_rows(group, parity):
    if CLASSES == 1:
        return rows_at(group)
    return pl.ds(group * 8 * CLASSES + parity, 8, stride=CLASSES)


def enter_kernel(parity, field_ref, own_ref, other_ref, out_ref):
    def step(group, carry):
        rows = natural_rows(group, parity)
        blocks = []
        for pair in range(BLOCKS // 2):
            cols = pl.ds(pair * LANES, LANES)
            blocks += pack(field_ref[0, rows, cols], field_ref[1, rows, cols])
        for block, value in enumerate(along_lanes(blocks, own_ref, other_ref)):
            out_ref[block, rows_at(group), :] = value
        return carry

    lax.fori_loop(0, out_ref.shape[1] // 8, step, 0)


def column_kernel(in_ref, out_ref, held):
    height = in_ref.shape[1]
    unit = height // BLOCKS

    def forward(group, carry):
        spectrum = small_dft([in_ref[r, rows_at(group), :] for r in range(BLOCKS)], -1)
        for freq, value in enumerate(spectrum):
            shift = shift_of(freq)
            turned_value = times_i(value)
            for copy, gain in enumerate((chirp_gain(BLOCKS - shift), chirp_gain(-shift))):
                held[freq, pl.ds(pl.multiple_of(group * 8 + copy * height, 8), 8), :] = (
                    value * np.float32(gain.real) + turned_value * np.float32(gain.imag)
                )
        return carry

    lax.fori_loop(0, height // 8, forward, 0)

    for group in range(height // 8):
        blocks = []
        for freq in range(BLOCKS):
            start = group * 8 + height - unit * shift_of(freq)
            blocks.append(held[freq, pl.ds(start, 8), :])
        for block, value in enumerate(small_dft(blocks, 1)):
            out_ref[block, rows_at(group), :] = value


def turn_kernel(parity, first_ref, wave_ref, t_ref, loss_ref, own_ref, other_ref, out_ref):
    use_loss = first_ref[0] == 1

    def step(group, carry):
        rows = natural_rows(group, parity)
        blocks = []
        for pair in range(BLOCKS // 2):
            cols = pl.ds(pair * LANES, LANES)
            real, imag = unpack(
                wave_ref[2 * pair, rows_at(group), :], wave_ref[2 * pair + 1, rows_at(group), :]
            )
            t_real, t_imag = t_ref[0, rows, cols], t_ref[1, rows, cols]
            pass_real = real * t_real + imag * t_imag
            pass_imag = imag * t_real - real * t_imag
            pass_real = jnp.where(use_loss, loss_ref[0, rows, cols], pass_real)
            pass_imag = jnp.where(use_loss, loss_ref[1, rows, cols], pass_imag)
            blocks += pack(pass_real, pass_imag)
        for block, value in enumerate(along_lanes(blocks, own_ref, other_ref)):
            out_ref[block, rows_at(group), :] = value
        return carry

    lax.fori_loop(0, out_ref.shape[1] // 8, step, 0)


def products_kernel(plain, lit_x_ref, lit_y_ref, field_ref, *refs):
    if plain:
        t_ref, *refs = refs
    wave_refs, out_refs = refs[:CLASSES], refs[CLASSES:]

    def step(group, carry):
        for parity, wave_ref in enumerate(wave_refs):
            rows = natural_rows(group, parity)
            y_real, y_imag = lit_y_ref[0, rows, :], lit_y_ref[1, rows, :]
            for pair in range(BLOCKS // 2):
                cols = pl.ds(pair * LANES, LANES)
                real, imag = unpack(
                    wave_ref[2 * pair, rows_at(group), :],
                    wave_ref[2 * pair + 1, rows_at(group), :],
                )
                if plain:
                    t_real, t_imag = t_ref[0, rows, cols], t_ref[1, rows, cols]
                    out_refs[1][0, rows, cols] = real * t_real + imag * t_imag
                    out_refs[1][1, rows, cols] = imag * t_real - real * t_imag
                x_real, x_imag = lit_x_ref[0:1, cols], lit_x_ref[1:2, cols]
                e_real = x_real * y_real - x_imag * y_imag
                e_imag = x_real * y_imag + x_imag * y_real
                f_real, f_imag = field_ref[0, rows, cols], field_ref[1, rows, cols]
                l_real = f_real * e_real - f_imag * e_imag
                l_imag = f_real * e_imag + f_imag * e_real
                out_refs[0][0, rows, cols] = real * l_real + imag * l_imag
                out_refs[0][1, rows, cols] = imag * l_real - real * l_imag
        return carry

    lax.fori_loop(0, WIDTH // 8 // CLASSES, step, 0)


WHOLE = pl.BlockSpec(memory_space=pltpu.VMEM)
SCALAR = pl.BlockSpec(memory_space=pltpu.SMEM)
HEIGHT = WIDTH // CLASSES
PACKED = jax.ShapeDtypeStruct((BLOCKS, HEIGHT, LANES), jnp.float32)
FIELD = jax.ShapeDtypeStruct((2, WIDTH, N), jnp.float32)


def call(kernel, out_shape, operands, name, scratch=(), scalars=0):
    outs = jax.tree.leaves(out_shape)
    size = sum(4 * math.prod(x.shape) for x in outs) + sum(4 * x.size for x in operands)
    return pl.pallas_call(
        kernel,
        out_shape=out_shape,
        in_specs=[SCALAR] * scalars + [WHOLE] * (len(operands) - scalars),
        out_specs=jax.tree.map(lambda _: WHOLE, out_shape),
        scratch_shapes=list(scratch),
        compiler_params=pltpu.CompilerParams(vmem_limit_bytes=VMEM_LIMIT),
        cost_estimate=pl.CostEstimate(flops=20 * size, bytes_accessed=size, transcendentals=0),
        name=name,
    )(*operands)


def exchange(packed):
    return lax.all_to_all(packed, "rows", split_axis=0, concat_axis=0, tiled=True)


def along_columns(packed):
    return call(
        column_kernel,
        PACKED,
        [packed],
        "columns",
        scratch=[pltpu.VMEM((BLOCKS, 2 * HEIGHT, LANES), jnp.float32)],
    )


def to_previous(value):
    count = lax.axis_size("depth")
    return lax.ppermute(value, "depth", [(s, (s - 1) % count) for s in range(count)])


def light(led_number, row_start):
    shift_col = led_number // LED_SIDE - LED_SIDE // 2
    shift_row = led_number % LED_SIDE - LED_SIDE // 2
    cols = shift_col * jnp.arange(N, dtype=jnp.int32) % N
    rows = shift_row * (row_start + jnp.arange(WIDTH, dtype=jnp.int32)) % N
    angle_x = 2.0 * math.pi / N * cols.astype(jnp.float32)
    angle_y = 2.0 * math.pi / N * rows.astype(jnp.float32)
    lit_x = jnp.stack([jnp.cos(angle_x), jnp.sin(angle_x)])
    lit_y = jnp.stack([jnp.cos(angle_y), jnp.sin(angle_y)])
    return lit_x, jnp.broadcast_to(lit_y[:, :, None], (2, WIDTH, LANES))


def per_device(grad_arriving, loss_grad, t_entry, t_exit, fields_entry, fields_exit, led_index):
    own, other = (jnp.asarray(table) for table in lane_tables())
    row_start = lax.axis_index("rows") * WIDTH
    first = (lax.axis_index("depth") == 0).astype(jnp.int32).reshape(1)
    waves, packed = [], []
    for parity in range(CLASSES):
        sent = call(
            functools.partial(enter_kernel, parity),
            PACKED,
            [grad_arriving[0], own, other],
            "enter",
        )
        waves.append(exchange(along_columns(exchange(sent))))
    for parity in range(CLASSES):
        packed.append(
            call(
                functools.partial(turn_kernel, parity),
                PACKED,
                [first, waves[parity], t_entry[0], loss_grad, own, other],
                "turn",
                scalars=1,
            )
        )
    grad_entry = call(
        functools.partial(products_kernel, False),
        FIELD,
        [*light(led_index[0, 0], row_start), fields_entry[0], *waves],
        "products",
    )
    seconds = [exchange(along_columns(exchange(to_previous(value)))) for value in packed]
    grad_exit, leaving = call(
        functools.partial(products_kernel, True),
        (FIELD, FIELD),
        [*light(led_index[0, 1], row_start), fields_exit[0], t_exit[0], *seconds],
        "products",
    )
    return (grad_entry[None], grad_exit[None], leaving[None])


def solution(mesh):
    spread = P("depth", None, "rows", None)
    return jax.shard_map(
        per_device,
        mesh=mesh,
        in_specs=(spread, P(None, "rows", None), spread, spread, spread, spread, P("depth", None)),
        out_specs=(spread, spread, spread),
        check_vma=False,
    )
```

```python
import functools
import math

import jax
import jax.numpy as jnp
import numpy as np
from jax import lax
from jax.experimental import pallas as pl
from jax.experimental.pallas import tpu as pltpu
from jax.sharding import PartitionSpec as P

LED_SIDE = 15
SPREAD = 3
BLOCKS = 32
N = 2048
WIDTH = N // BLOCKS
LANES = 2 * WIDTH
HALF = WIDTH // 4
TILES = HALF // 8
VMEM_LIMIT = 24 * 1024 * 1024

INVERSE = pow(SPREAD, -1, N)
_k = np.arange(N, dtype=np.int64)
GAUSS = np.exp(-2j * np.pi * ((SPREAD * _k * _k) % N) / N).sum() / N


def chirp_gain(distance):
    return complex(GAUSS * np.exp(2j * np.pi * ((INVERSE * distance * distance) % N) / N))


def shift_of(freq):
    return SPREAD * (freq - BLOCKS // 2) % BLOCKS


def plus(a, b):
    return (a[0] + b[0], a[1] + b[1])


def minus(a, b):
    return (a[0] - b[0], a[1] - b[1])


def times_i(a):
    return (-a[1], a[0])


def times(a, real, imag):
    return (a[0] * real - a[1] * imag, a[0] * imag + a[1] * real)


def scaled(a, factor):
    return times(a, np.float32(factor.real), np.float32(factor.imag))


def turned(a, step, count, sign):
    step = step * sign % count
    if step == 0:
        return a
    if 2 * step == count:
        return (-a[0], -a[1])
    if 4 * step == count:
        return times_i(a)
    if 4 * step == 3 * count:
        return (a[1], -a[0])
    if 8 * step % count == 0:
        root = np.float32(math.sqrt(0.5))
        eighth = 8 * step // count
        added, taken = (a[0] + a[1]) * root, (a[0] - a[1]) * root
        return {
            1: (taken, added),
            3: (-added, taken),
            5: (-taken, -added),
            7: (added, -taken),
        }[eighth]
    angle = 2.0 * math.pi * step / count
    return scaled(a, complex(math.cos(angle), math.sin(angle)))


def small_dft(values, sign):
    count = len(values)
    if count == 1:
        return values
    if count == 2:
        return [plus(*values), minus(*values)]
    quarter = count // 4
    parts = [small_dft(values[phase::4], sign) for phase in range(4)]
    result = [None] * count
    for j in range(quarter):
        a, b, c, d = (turned(parts[k][j], j * k, count, sign) for k in range(4))
        sum_ac, dif_ac, sum_bd, dif_bd = plus(a, c), minus(a, c), plus(b, d), minus(b, d)
        result[j] = plus(sum_ac, sum_bd)
        result[j + 2 * quarter] = minus(sum_ac, sum_bd)
        up = (dif_ac[0] - dif_bd[1], dif_ac[1] + dif_bd[0])
        down = (dif_ac[0] + dif_bd[1], dif_ac[1] - dif_bd[0])
        result[j + quarter], result[j + 3 * quarter] = (up, down) if sign > 0 else (down, up)
    return result


def lane_ids():
    return lax.broadcasted_iota(jnp.int32, (8, LANES), 1)


def halves(first, second):
    low = lane_ids() < WIDTH
    return (
        jnp.where(low, first, pltpu.roll(second, WIDTH, 1)),
        jnp.where(low, pltpu.roll(first, WIDTH, 1), second),
    )


def tile(index):
    return pl.ds(8 * index, 8)


def get(ref, block, rows):
    return (ref[block, 0, rows, :], ref[block, 1, rows, :])


def put(ref, block, rows, value):
    ref[block, 0, rows, :] = value[0]
    ref[block, 1, rows, :] = value[1]


def block_dft(load, emit, stage, rows, sign):
    for k in range(4):
        for j, value in enumerate(small_dft([load(4 * n + k) for n in range(8)], sign)):
            put(stage, 8 * k + j, rows, turned(value, j * k, BLOCKS, sign))
    for j in range(8):
        outs = small_dft([get(stage, 8 * k + j, rows) for k in range(4)], sign)
        for step, value in enumerate(outs):
            emit(j + 8 * step, value)


def along_lanes(load, out_ref, stage, moved):
    inside = lane_ids() % WIDTH
    for index in range(TILES):
        rows = tile(index)

        def move(freq, value):
            shift = 2 * shift_of(freq)
            if shift:
                mask = inside >= shift
                value = tuple(
                    jnp.where(mask, pltpu.roll(v, shift, 1), pltpu.roll(v, shift + WIDTH, 1))
                    for v in value
                )
                plain, wrapped = chirp_gain(-(shift // 2)), chirp_gain(BLOCKS - shift // 2)
                real = jnp.where(mask, np.float32(plain.real), np.float32(wrapped.real))
                imag = jnp.where(mask, np.float32(plain.imag), np.float32(wrapped.imag))
                value = times(value, real, imag)
            else:
                value = scaled(value, chirp_gain(0))
            put(moved, freq, rows, value)

        block_dft(functools.partial(load, index), move, stage, rows, -1)
        block_dft(
            lambda freq: get(moved, freq, rows),
            lambda block, value: put(out_ref, block, rows, value),
            stage,
            rows,
            1,
        )


def split_rows(read, parity_outs, apart):
    for pair in range(BLOCKS // 2):
        for part in range(2):
            for quarter in range(4):
                slot = (pair * 2 + part) * 4 + quarter
                apart[slot] = read(part, quarter, pl.ds(pair * LANES, LANES))
    for parity, out in parity_outs:
        for pair in range(BLOCKS // 2):
            for part in range(2):
                slot = (pair * 2 + part) * 4
                for index in range(TILES):
                    upper, lower = (
                        apart[slot + index + TILES * half, pl.ds(parity, 8, stride=2), :]
                        for half in range(2)
                    )
                    left, right = halves(upper, lower)
                    out[2 * pair, part, tile(index), :] = left
                    out[2 * pair + 1, part, tile(index), :] = right


def enter_kernel(parity, field_ref, out_ref, apart, packed, stage, moved):
    def read(part, quarter, cols):
        return field_ref[part, pl.ds(16 * quarter, 16), cols]

    split_rows(read, [(parity, packed)], apart)
    along_lanes(
        lambda index, block: get(packed, block, tile(index)), out_ref, stage, moved
    )


def gather_kernel(first_ref, t_ref, loss_ref, even_ref, odd_ref, apart):
    use_loss = first_ref[0] == 1

    def read_from(ref):
        return lambda part, quarter, cols: ref[part, pl.ds(16 * quarter, 16), cols]

    @pl.when(use_loss)
    def _():
        split_rows(read_from(loss_ref), [(0, even_ref), (1, odd_ref)], apart)

    @pl.when(jnp.logical_not(use_loss))
    def _():
        split_rows(read_from(t_ref), [(0, even_ref), (1, odd_ref)], apart)


def turn_kernel(first_ref, wave_ref, other_ref, out_ref, stage, moved):
    use_loss = first_ref[0] == 1

    def load(index, block):
        real, imag = get(wave_ref, block, tile(index))
        t_real, t_imag = get(other_ref, block, tile(index))
        return (
            jnp.where(use_loss, t_real, real * t_real + imag * t_imag),
            jnp.where(use_loss, t_imag, imag * t_real - real * t_imag),
        )

    along_lanes(load, out_ref, stage, moved)


def column_kernel(in_ref, out_ref, stage, held):
    low = lane_ids() < WIDTH
    for index in range(TILES):
        rows = tile(index)

        def hold(freq, value):
            shift = shift_of(freq)
            plain = scaled(value, chirp_gain(-shift))
            wrapped = scaled(value, chirp_gain(BLOCKS - shift)) if shift else None
            if shift > HALF:
                put(held, freq, rows, wrapped)
            if shift < HALF:
                put(held, freq, pl.ds(2 * HALF + 8 * index, 8), plain)
            if shift:
                crossed = tuple(
                    pltpu.roll(jnp.where(low, p, w), WIDTH, 1) for p, w in zip(plain, wrapped)
                )
                put(held, freq, pl.ds(HALF + 8 * index, 8), crossed)

        block_dft(lambda block: get(in_ref, block, rows), hold, stage, rows, -1)
    for index in range(TILES):
        rows = tile(index)
        block_dft(
            lambda freq: get(held, freq, pl.ds(2 * HALF - shift_of(freq) + 8 * index, 8)),
            lambda block, value: put(out_ref, block, rows, value),
            stage,
            rows,
            1,
        )


def products_kernel(plain, lit_x_ref, lit_y_ref, field_ref, *refs):
    if plain:
        t_ref, *refs = refs
    even_ref, odd_ref, *out_refs, whole = refs
    for pair in range(BLOCKS // 2):
        for part in range(2):
            for parity, wave_ref in enumerate((even_ref, odd_ref)):
                for index in range(TILES):
                    upper, lower = halves(
                        wave_ref[2 * pair, part, tile(index), :],
                        wave_ref[2 * pair + 1, part, tile(index), :],
                    )
                    for half, value in enumerate((upper, lower)):
                        start = 16 * (index + TILES * half) + parity
                        whole[2 * pair + part, pl.ds(start, 8, stride=2), :] = value

    def step(group, carry):
        rows = pl.ds(pl.multiple_of(8 * group, 8), 8)
        y_real, y_imag = lit_y_ref[0, rows, :], lit_y_ref[1, rows, :]
        for pair in range(BLOCKS // 2):
            cols = pl.ds(pair * LANES, LANES)
            real, imag = whole[2 * pair, rows, :], whole[2 * pair + 1, rows, :]
            if plain:
                t_real, t_imag = t_ref[0, rows, cols], t_ref[1, rows, cols]
                out_refs[1][0, rows, cols] = real * t_real + imag * t_imag
                out_refs[1][1, rows, cols] = imag * t_real - real * t_imag
            x_real, x_imag = lit_x_ref[0:1, cols], lit_x_ref[1:2, cols]
            e_real = x_real * y_real - x_imag * y_imag
            e_imag = x_real * y_imag + x_imag * y_real
            f_real, f_imag = field_ref[0, rows, cols], field_ref[1, rows, cols]
            l_real = f_real * e_real - f_imag * e_imag
            l_imag = f_real * e_imag + f_imag * e_real
            out_refs[0][0, rows, cols] = real * l_real + imag * l_imag
            out_refs[0][1, rows, cols] = imag * l_real - real * l_imag
        return carry

    lax.fori_loop(0, WIDTH // 8, step, 0)


WHOLE = pl.BlockSpec(memory_space=pltpu.VMEM)
SCALAR = pl.BlockSpec(memory_space=pltpu.SMEM)
CHAIN = (BLOCKS, 2, HALF, LANES)
PACKED = jax.ShapeDtypeStruct(CHAIN, jnp.float32)
FIELD = jax.ShapeDtypeStruct((2, WIDTH, N), jnp.float32)
BUFFER = pltpu.VMEM(CHAIN, jnp.float32)
APART = pltpu.VMEM((8 * BLOCKS // 2, 16, LANES), jnp.float32)


def call(kernel, out_shape, operands, name, scratch=(), scalars=0):
    outs = jax.tree.leaves(out_shape)
    size = sum(4 * math.prod(x.shape) for x in outs) + sum(4 * x.size for x in operands)
    return pl.pallas_call(
        kernel,
        out_shape=out_shape,
        in_specs=[SCALAR] * scalars + [WHOLE] * (len(operands) - scalars),
        out_specs=jax.tree.map(lambda _: WHOLE, out_shape),
        scratch_shapes=list(scratch),
        compiler_params=pltpu.CompilerParams(vmem_limit_bytes=VMEM_LIMIT),
        cost_estimate=pl.CostEstimate(flops=20 * size, bytes_accessed=size, transcendentals=0),
        name=name,
    )(*operands)


def exchange(packed):
    return lax.all_to_all(packed, "rows", split_axis=0, concat_axis=0, tiled=True)


def along_columns(packed):
    held = pltpu.VMEM((BLOCKS, 2, 3 * HALF, LANES), jnp.float32)
    return call(column_kernel, PACKED, [packed], "columns", scratch=[BUFFER, held])


def to_previous(value):
    count = lax.axis_size("depth")
    return lax.ppermute(value, "depth", [(s, (s - 1) % count) for s in range(count)])


def light(led_number, row_start):
    shift_col = led_number // LED_SIDE - LED_SIDE // 2
    shift_row = led_number % LED_SIDE - LED_SIDE // 2
    cols = shift_col * jnp.arange(N, dtype=jnp.int32) % N
    rows = shift_row * (row_start + jnp.arange(WIDTH, dtype=jnp.int32)) % N
    angle_x = 2.0 * math.pi / N * cols.astype(jnp.float32)
    angle_y = 2.0 * math.pi / N * rows.astype(jnp.float32)
    lit_x = jnp.stack([jnp.cos(angle_x), jnp.sin(angle_x)])
    lit_y = jnp.stack([jnp.cos(angle_y), jnp.sin(angle_y)])
    return lit_x, jnp.broadcast_to(lit_y[:, :, None], (2, WIDTH, LANES))


def products(plain, operands):
    return call(
        functools.partial(products_kernel, plain),
        (FIELD, FIELD) if plain else FIELD,
        operands,
        "products",
        scratch=[pltpu.VMEM((BLOCKS, WIDTH, LANES), jnp.float32)],
    )


def per_device(grad_arriving, loss_grad, t_entry, t_exit, fields_entry, fields_exit, led_index):
    row_start = lax.axis_index("rows") * WIDTH
    first = (lax.axis_index("depth") == 0).astype(jnp.int32).reshape(1)
    others = call(
        gather_kernel, (PACKED, PACKED), [first, t_entry[0], loss_grad], "gather", [APART], 1
    )
    firsts, seconds = [], []
    for parity in range(2):
        sent = call(
            functools.partial(enter_kernel, parity),
            PACKED,
            [grad_arriving[0]],
            "enter",
            scratch=[APART, BUFFER, BUFFER, BUFFER],
        )
        firsts.append(exchange(along_columns(exchange(sent))))
    for parity in range(2):
        sent = call(
            turn_kernel,
            PACKED,
            [first, firsts[parity], others[parity]],
            "turn",
            scratch=[BUFFER, BUFFER],
            scalars=1,
        )
        if parity == 0:
            returned = along_columns(exchange(to_previous(sent)))
        else:
            returned = to_previous(along_columns(exchange(sent)))
        seconds.append(exchange(returned))
    grad_entry = products(
        False, [*light(led_index[0, 0], row_start), fields_entry[0], *firsts]
    )
    grad_exit, leaving = products(
        True, [*light(led_index[0, 1], row_start), fields_exit[0], t_exit[0], *seconds]
    )
    return (grad_entry[None], grad_exit[None], leaving[None])


def solution(mesh):
    spread = P("depth", None, "rows", None)
    return jax.shard_map(
        per_device,
        mesh=mesh,
        in_specs=(spread, P(None, "rows", None), spread, spread, spread, spread, P("depth", None)),
        out_specs=(spread, spread, spread),
        check_vma=False,
    )
```

```python
import functools
import math

import jax
import jax.numpy as jnp
import numpy as np
from jax import lax
from jax.experimental import pallas as pl
from jax.experimental.pallas import tpu as pltpu
from jax.sharding import PartitionSpec as P

LED_SIDE = 15
SPREAD = 3
BLOCKS = 32
N = 2048
WIDTH = N // BLOCKS
LANES = 2 * WIDTH
HALF = WIDTH // 2
TILES = HALF // 8
VMEM_LIMIT = 24 * 1024 * 1024

INVERSE = pow(SPREAD, -1, N)
_k = np.arange(N, dtype=np.int64)
GAUSS = np.exp(-2j * np.pi * ((SPREAD * _k * _k) % N) / N).sum() / N


def chirp_gain(distance):
    return complex(GAUSS * np.exp(2j * np.pi * ((INVERSE * distance * distance) % N) / N))


def shift_of(freq):
    pairs = SPREAD * (freq - BLOCKS // 2) % BLOCKS
    return 2 * pairs, chirp_gain(-pairs), chirp_gain(BLOCKS - pairs)


def plus(a, b):
    return (a[0] + b[0], a[1] + b[1])


def minus(a, b):
    return (a[0] - b[0], a[1] - b[1])


def times_i(a):
    return (-a[1], a[0])


def times(a, real, imag):
    return (a[0] * real - a[1] * imag, a[0] * imag + a[1] * real)


def scaled(a, factor):
    return times(a, np.float32(factor.real), np.float32(factor.imag))


def turned(a, step, count, sign):
    step = step * sign % count
    if step == 0:
        return a
    if 2 * step == count:
        return (-a[0], -a[1])
    if 4 * step == count:
        return times_i(a)
    if 4 * step == 3 * count:
        return (a[1], -a[0])
    if 8 * step % count == 0:
        root = np.float32(math.sqrt(0.5))
        eighth = 8 * step // count
        added, taken = (a[0] + a[1]) * root, (a[0] - a[1]) * root
        return {
            1: (taken, added),
            3: (-added, taken),
            5: (-taken, -added),
            7: (added, -taken),
        }[eighth]
    angle = 2.0 * math.pi * step / count
    return scaled(a, complex(math.cos(angle), math.sin(angle)))


def small_dft(values, sign):
    count = len(values)
    if count == 1:
        return values
    if count == 2:
        return [plus(*values), minus(*values)]
    quarter = count // 4
    parts = [small_dft(values[phase::4], sign) for phase in range(4)]
    result = [None] * count
    for j in range(quarter):
        a, b, c, d = (turned(parts[k][j], j * k, count, sign) for k in range(4))
        sum_ac, dif_ac, sum_bd, dif_bd = plus(a, c), minus(a, c), plus(b, d), minus(b, d)
        result[j] = plus(sum_ac, sum_bd)
        result[j + 2 * quarter] = minus(sum_ac, sum_bd)
        up = (dif_ac[0] - dif_bd[1], dif_ac[1] + dif_bd[0])
        down = (dif_ac[0] + dif_bd[1], dif_ac[1] - dif_bd[0])
        result[j + quarter], result[j + 3 * quarter] = (up, down) if sign > 0 else (down, up)
    return result


def lane_ids():
    return lax.broadcasted_iota(jnp.int32, (8, LANES), 1)


def halves(first, second):
    low = lane_ids() < WIDTH
    return (
        jnp.where(low, first, pltpu.roll(second, WIDTH, 1)),
        jnp.where(low, pltpu.roll(first, WIDTH, 1), second),
    )


def tile(index):
    return pl.ds(8 * index, 8)


def get(ref, block, rows):
    return (ref[block, 0, rows, :], ref[block, 1, rows, :])


def put(ref, block, rows, value):
    ref[block, 0, rows, :] = value[0]
    ref[block, 1, rows, :] = value[1]


def block_dft(load, emit, stage, rows, sign):
    for k in range(4):
        for j, value in enumerate(small_dft([load(4 * n + k) for n in range(8)], sign)):
            put(stage, 8 * k + j, rows, turned(value, j * k, BLOCKS, sign))
    for j in range(8):
        outs = small_dft([get(stage, 8 * k + j, rows) for k in range(4)], sign)
        for step, value in enumerate(outs):
            emit(j + 8 * step, value)


def along_lanes(load, store, stage, moved):
    inside = lane_ids() % WIDTH
    for index in range(TILES):
        rows = tile(index)

        def move(freq, value):
            shift, plain, wrapped = shift_of(freq)
            if shift:
                mask = inside >= shift
                value = tuple(
                    jnp.where(mask, pltpu.roll(v, shift, 1), pltpu.roll(v, shift + WIDTH, 1))
                    for v in value
                )
                real = jnp.where(mask, np.float32(plain.real), np.float32(wrapped.real))
                imag = jnp.where(mask, np.float32(plain.imag), np.float32(wrapped.imag))
                value = times(value, real, imag)
            else:
                value = scaled(value, plain)
            put(moved, freq, rows, value)

        block_dft(functools.partial(load, index), move, stage, rows, -1)
        block_dft(
            lambda freq: get(moved, freq, rows), functools.partial(store, index), stage, rows, 1
        )


def along_rows(load, store, stage, held):
    low = lane_ids() < WIDTH
    for index in range(TILES):
        rows = tile(index)

        def hold(freq, value):
            shift, plain, wrapped = shift_of(freq)
            plain = scaled(value, plain)
            wrapped = scaled(value, wrapped) if shift else None
            if shift > HALF:
                put(held, freq, rows, wrapped)
            if shift < HALF:
                put(held, freq, pl.ds(2 * HALF + 8 * index, 8), plain)
            if shift:
                crossed = tuple(
                    pltpu.roll(jnp.where(low, p, w), WIDTH, 1) for p, w in zip(plain, wrapped)
                )
                put(held, freq, pl.ds(HALF + 8 * index, 8), crossed)

        block_dft(functools.partial(load, index), hold, stage, rows, -1)
    for index in range(TILES):
        block_dft(
            lambda freq: get(held, freq, pl.ds(2 * HALF - shift_of(freq)[0] + 8 * index, 8)),
            functools.partial(store, index),
            stage,
            tile(index),
            1,
        )


def natural(index, half):
    return pl.ds(8 * index + HALF * half, 8)


def read_pair(ref, index, pair):
    cols = pl.ds(pair * LANES, LANES)
    parts = [
        halves(ref[part, natural(index, 0), cols], ref[part, natural(index, 1), cols])
        for part in range(2)
    ]
    return [(parts[0][side], parts[1][side]) for side in range(2)]


def read_field(ref, write):
    for index in range(TILES):
        for pair in range(BLOCKS // 2):
            for side, value in enumerate(read_pair(ref, index, pair)):
                write(index, 2 * pair + side, value)


def enter_kernel(first_ref, field_ref, t_ref, loss_ref, out_ref, packed, stage, moved):
    read_field(field_ref, lambda index, block, value: put(packed, block, tile(index), value))
    along_lanes(
        lambda index, block: get(packed, block, tile(index)),
        lambda index, block, value: put(out_ref.at[:, 0], block, tile(index), value),
        stage,
        moved,
    )

    def other(index, block, value):
        put(out_ref.at[:, 1], block, tile(index), value)

    @pl.when(first_ref[0] == 1)
    def _():
        read_field(loss_ref, other)

    @pl.when(first_ref[0] != 1)
    def _():
        read_field(t_ref, other)


def column_kernel(first_ref, in_ref, wave_ref, out_ref, stage, held):
    use_loss = first_ref[0] == 1
    along_rows(
        lambda index, block: get(in_ref.at[:, 0], block, tile(index)),
        lambda index, block, value: put(wave_ref, block, tile(index), value),
        stage,
        held,
    )

    def passing(index, block):
        real, imag = get(wave_ref, block, tile(index))
        t_real, t_imag = get(in_ref.at[:, 1], block, tile(index))
        return (
            jnp.where(use_loss, t_real, real * t_real + imag * t_imag),
            jnp.where(use_loss, t_imag, imag * t_real - real * t_imag),
        )

    along_rows(
        passing,
        lambda index, block, value: put(out_ref, block, tile(index), value),
        stage,
        held,
    )


def write_products(wave, lit_x_ref, lit_y_ref, field_ref, out_ref, t_ref=None, plain_ref=None):
    for index in range(TILES):
        lit_y = [
            (lit_y_ref[0, natural(index, half), :], lit_y_ref[1, natural(index, half), :])
            for half in range(2)
        ]
        for pair in range(BLOCKS // 2):
            cols = pl.ds(pair * LANES, LANES)
            left, right = wave(index, 2 * pair), wave(index, 2 * pair + 1)
            reals, imags = halves(left[0], right[0]), halves(left[1], right[1])
            lit_x = (lit_x_ref[0:1, cols], lit_x_ref[1:2, cols])
            for half in range(2):
                rows = natural(index, half)
                real, imag = reals[half], imags[half]
                if t_ref is not None:
                    t_real, t_imag = t_ref[0, rows, cols], t_ref[1, rows, cols]
                    plain_ref[0, rows, cols] = real * t_real + imag * t_imag
                    plain_ref[1, rows, cols] = imag * t_real - real * t_imag
                lit = times(lit_y[half], *lit_x)
                f_real, f_imag = times(lit, field_ref[0, rows, cols], field_ref[1, rows, cols])
                out_ref[0, rows, cols] = real * f_real + imag * f_imag
                out_ref[1, rows, cols] = imag * f_real - real * f_imag


def entry_kernel(lit_x_ref, lit_y_ref, field_ref, wave_ref, out_ref):
    write_products(
        lambda index, block: get(wave_ref, block, tile(index)),
        lit_x_ref,
        lit_y_ref,
        field_ref,
        out_ref,
    )


def exit_kernel(
    lit_x_ref, lit_y_ref, field_ref, t_ref, in_ref, out_ref, plain_ref, packed, stage, moved
):
    along_lanes(
        lambda index, block: get(in_ref, block, tile(index)),
        lambda index, block, value: put(packed, block, tile(index), value),
        stage,
        moved,
    )
    write_products(
        lambda index, block: get(packed, block, tile(index)),
        lit_x_ref,
        lit_y_ref,
        field_ref,
        out_ref,
        t_ref,
        plain_ref,
    )


WHOLE = pl.BlockSpec(memory_space=pltpu.VMEM)
SCALAR = pl.BlockSpec(memory_space=pltpu.SMEM)
CHAIN = (BLOCKS, 2, HALF, LANES)
PACKED = jax.ShapeDtypeStruct(CHAIN, jnp.float32)
BOTH = jax.ShapeDtypeStruct((BLOCKS, 2, 2, HALF, LANES), jnp.float32)
FIELD = jax.ShapeDtypeStruct((2, WIDTH, N), jnp.float32)
BUFFER = pltpu.VMEM(CHAIN, jnp.float32)
HELD = pltpu.VMEM((BLOCKS, 2, 3 * HALF, LANES), jnp.float32)


def call(kernel, out_shape, operands, name, scratch=(), scalars=0):
    outs = jax.tree.leaves(out_shape)
    size = sum(4 * math.prod(x.shape) for x in outs) + sum(4 * x.size for x in operands)
    return pl.pallas_call(
        kernel,
        out_shape=out_shape,
        in_specs=[SCALAR] * scalars + [WHOLE] * (len(operands) - scalars),
        out_specs=jax.tree.map(lambda _: WHOLE, out_shape),
        scratch_shapes=list(scratch),
        compiler_params=pltpu.CompilerParams(vmem_limit_bytes=VMEM_LIMIT),
        cost_estimate=pl.CostEstimate(flops=20 * size, bytes_accessed=size, transcendentals=0),
        name=name,
    )(*operands)


def exchange(packed):
    return lax.all_to_all(packed, "rows", split_axis=0, concat_axis=0, tiled=True)


def to_previous(value):
    count = lax.axis_size("depth")
    return lax.ppermute(value, "depth", [(s, (s - 1) % count) for s in range(count)])


def light(led_number, row_start):
    shift_col = led_number // LED_SIDE - LED_SIDE // 2
    shift_row = led_number % LED_SIDE - LED_SIDE // 2
    cols = shift_col * jnp.arange(N, dtype=jnp.int32) % N
    rows = shift_row * (row_start + jnp.arange(WIDTH, dtype=jnp.int32)) % N
    angle_x = 2.0 * math.pi / N * cols.astype(jnp.float32)
    angle_y = 2.0 * math.pi / N * rows.astype(jnp.float32)
    lit_x = jnp.stack([jnp.cos(angle_x), jnp.sin(angle_x)])
    lit_y = jnp.stack([jnp.cos(angle_y), jnp.sin(angle_y)])
    return lit_x, jnp.broadcast_to(lit_y[:, :, None], (2, WIDTH, LANES))


def per_device(grad_arriving, loss_grad, t_entry, t_exit, fields_entry, fields_exit, led_index):
    row_start = lax.axis_index("rows") * WIDTH
    first = (lax.axis_index("depth") == 0).astype(jnp.int32).reshape(1)
    both = call(
        enter_kernel,
        BOTH,
        [first, grad_arriving[0], t_entry[0], loss_grad],
        "enter",
        [BUFFER, BUFFER, BUFFER],
        1,
    )
    wave, onward = call(
        column_kernel, (PACKED, PACKED), [first, exchange(both)], "columns", [BUFFER, HELD], 1
    )
    onward = to_previous(onward)
    wave = exchange(wave)
    grad_entry = call(
        entry_kernel,
        FIELD,
        [*light(led_index[0, 0], row_start), fields_entry[0], wave],
        "entry",
    )
    grad_exit, leaving = call(
        exit_kernel,
        (FIELD, FIELD),
        [
            *light(led_index[0, 1], row_start),
            fields_exit[0],
            t_exit[0],
            exchange(onward),
        ],
        "exit",
        [BUFFER, BUFFER, BUFFER],
    )
    return (grad_entry[None], grad_exit[None], leaving[None])


def solution(mesh):
    spread = P("depth", None, "rows", None)
    return jax.shard_map(
        per_device,
        mesh=mesh,
        in_specs=(spread, P(None, "rows", None), spread, spread, spread, spread, P("depth", None)),
        out_specs=(spread, spread, spread),
        check_vma=False,
    )
```

```python
import functools
import math

import jax
import jax.numpy as jnp
import numpy as np
from jax import lax
from jax.experimental import pallas as pl
from jax.experimental.pallas import tpu as pltpu
from jax.sharding import PartitionSpec as P

LED_SIDE = 15
SPREAD = 3
BLOCKS = 32
N = 2048
WIDTH = N // BLOCKS
LANES = 2 * WIDTH
HALF = WIDTH // 2
TILES = HALF // 8
VMEM_LIMIT = 24 * 1024 * 1024

INVERSE = pow(SPREAD, -1, N)
_k = np.arange(N, dtype=np.int64)
GAUSS = np.exp(-2j * np.pi * ((SPREAD * _k * _k) % N) / N).sum() / N


def chirp_gain(distance):
    return complex(GAUSS * np.exp(2j * np.pi * ((INVERSE * distance * distance) % N) / N))


def shift_of(freq):
    pairs = SPREAD * (freq - BLOCKS // 2) % BLOCKS
    return 2 * pairs, chirp_gain(-pairs), chirp_gain(BLOCKS - pairs)


def plus(a, b):
    return (a[0] + b[0], a[1] + b[1])


def minus(a, b):
    return (a[0] - b[0], a[1] - b[1])


def times_i(a):
    return (-a[1], a[0])


def times(a, real, imag):
    return (a[0] * real - a[1] * imag, a[0] * imag + a[1] * real)


def scaled(a, factor):
    return times(a, np.float32(factor.real), np.float32(factor.imag))


def turned(a, step, count, sign):
    step = step * sign % count
    if step == 0:
        return a
    if 2 * step == count:
        return (-a[0], -a[1])
    if 4 * step == count:
        return times_i(a)
    if 4 * step == 3 * count:
        return (a[1], -a[0])
    if 8 * step % count == 0:
        root = np.float32(math.sqrt(0.5))
        eighth = 8 * step // count
        added, taken = (a[0] + a[1]) * root, (a[0] - a[1]) * root
        return {
            1: (taken, added),
            3: (-added, taken),
            5: (-taken, -added),
            7: (added, -taken),
        }[eighth]
    angle = 2.0 * math.pi * step / count
    return scaled(a, complex(math.cos(angle), math.sin(angle)))


def small_dft(values, sign):
    count = len(values)
    if count == 1:
        return values
    if count == 2:
        return [plus(*values), minus(*values)]
    quarter = count // 4
    parts = [small_dft(values[phase::4], sign) for phase in range(4)]
    result = [None] * count
    for j in range(quarter):
        a, b, c, d = (turned(parts[k][j], j * k, count, sign) for k in range(4))
        sum_ac, dif_ac, sum_bd, dif_bd = plus(a, c), minus(a, c), plus(b, d), minus(b, d)
        result[j] = plus(sum_ac, sum_bd)
        result[j + 2 * quarter] = minus(sum_ac, sum_bd)
        up = (dif_ac[0] - dif_bd[1], dif_ac[1] + dif_bd[0])
        down = (dif_ac[0] + dif_bd[1], dif_ac[1] - dif_bd[0])
        result[j + quarter], result[j + 3 * quarter] = (up, down) if sign > 0 else (down, up)
    return result


def lane_ids():
    return lax.broadcasted_iota(jnp.int32, (8, LANES), 1)


def halves(first, second):
    low = lane_ids() < WIDTH
    return (
        jnp.where(low, first, pltpu.roll(second, WIDTH, 1)),
        jnp.where(low, pltpu.roll(first, WIDTH, 1), second),
    )


def tile(index):
    return pl.ds(8 * index, 8)


def get(ref, block, rows):
    return (ref[block, 0, rows, :], ref[block, 1, rows, :])


def put(ref, block, rows, value):
    ref[block, 0, rows, :] = value[0]
    ref[block, 1, rows, :] = value[1]


def block_dft(load, emit, stage, rows, sign):
    for k in range(4):
        for j, value in enumerate(small_dft([load(4 * n + k) for n in range(8)], sign)):
            put(stage, 8 * k + j, rows, turned(value, j * k, BLOCKS, sign))
    for j in range(8):
        outs = small_dft([get(stage, 8 * k + j, rows) for k in range(4)], sign)
        for step, value in enumerate(outs):
            emit(j + 8 * step, value)


def along_lanes(load, store, stage, moved):
    inside = lane_ids() % WIDTH
    for index in range(TILES):
        rows = tile(index)

        def move(freq, value):
            shift, plain, wrapped = shift_of(freq)
            if shift:
                mask = inside >= shift
                value = tuple(
                    jnp.where(mask, pltpu.roll(v, shift, 1), pltpu.roll(v, shift + WIDTH, 1))
                    for v in value
                )
                real = jnp.where(mask, np.float32(plain.real), np.float32(wrapped.real))
                imag = jnp.where(mask, np.float32(plain.imag), np.float32(wrapped.imag))
                value = times(value, real, imag)
            else:
                value = scaled(value, plain)
            put(moved, freq, rows, value)

        block_dft(functools.partial(load, index), move, stage, rows, -1)
        block_dft(
            lambda freq: get(moved, freq, rows), functools.partial(store, index), stage, rows, 1
        )


def along_rows(load, store, stage, held):
    low = lane_ids() < WIDTH
    for index in range(TILES):
        rows = tile(index)

        def hold(freq, value):
            shift, plain, wrapped = shift_of(freq)
            plain = scaled(value, plain)
            wrapped = scaled(value, wrapped) if shift else None
            if shift > HALF:
                put(held, freq, rows, wrapped)
            if shift < HALF:
                put(held, freq, pl.ds(2 * HALF + 8 * index, 8), plain)
            if shift:
                crossed = tuple(
                    pltpu.roll(jnp.where(low, p, w), WIDTH, 1) for p, w in zip(plain, wrapped)
                )
                put(held, freq, pl.ds(HALF + 8 * index, 8), crossed)

        block_dft(functools.partial(load, index), hold, stage, rows, -1)
    for index in range(TILES):
        block_dft(
            lambda freq: get(held, freq, pl.ds(2 * HALF - shift_of(freq)[0] + 8 * index, 8)),
            functools.partial(store, index),
            stage,
            tile(index),
            1,
        )


def natural(index, half):
    return pl.ds(8 * index + HALF * half, 8)


def field_copies(source, target, sems):
    return [
        [
            pltpu.make_async_copy(
                source.at[part, natural(index, half), :],
                target.at[part, natural(index, half), :],
                sems.at[index, part, half],
            )
            for part in range(2)
            for half in range(2)
        ]
        for index in range(TILES)
    ]


def start(copies):
    for tile_copies in copies:
        for copy in tile_copies:
            copy.start()


def wait(tile_copies):
    for copy in tile_copies:
        copy.wait()


def read_field(ref, index, write):
    for pair in range(BLOCKS // 2):
        cols = pl.ds(pair * LANES, LANES)
        parts = [
            halves(ref[part, natural(index, 0), cols], ref[part, natural(index, 1), cols])
            for part in range(2)
        ]
        for side in range(2):
            write(2 * pair + side, (parts[0][side], parts[1][side]))


def device_at(info_ref, order, sign, step, other, core):
    here = (info_ref[0], info_ref[1])
    near = (here[order] + sign * step) & 3
    far = (here[1 - order] + sign * other) & 3
    x, y = (near, far) if order == 0 else (far, near)
    return 8 * x + 2 * y + (info_ref[2] ^ core)


def deal(info_ref, order, blocks_ref, out_refs, rows=slice(None)):
    for step in range(4):
        for other in range(4):
            for core in range(2):
                block = device_at(info_ref, order, 1, step, other, core)
                out_refs[step][other, core] = blocks_ref[block, :, rows, :]


def collect(info_ref, order, in_refs, blocks_ref, rows=slice(None)):
    for other in range(4):
        for core in range(2):
            for step in range(4):
                block = device_at(info_ref, order, -1, step, other, core)
                blocks_ref[block, :, rows, :] = in_refs[2 * other + core][step]


def regroup_kernel(*refs):
    in_refs, out_refs = refs[:4], refs[4:]
    for other in range(4):
        for core in range(2):
            for step in range(4):
                out_refs[2 * other + core][step] = in_refs[step][other, core]


def other_kernel(info_ref, t_hbm, loss_hbm, *refs):
    out_refs, (field, blocks, sems) = refs[:4], refs[4:]
    use_loss = info_ref[3] == 1
    from_loss, from_t = (field_copies(hbm, field, sems) for hbm in (loss_hbm, t_hbm))

    @pl.when(use_loss)
    def _():
        start(from_loss)

    @pl.when(jnp.logical_not(use_loss))
    def _():
        start(from_t)

    for index in range(TILES):
        wait(from_t[index])
        read_field(
            field, index, lambda block, value: put(blocks, block, tile(index), value)
        )
    deal(info_ref, 1, blocks, out_refs)


def enter_kernel(info_ref, field_hbm, *refs):
    out_refs, (field, packed, stage, moved, sems) = refs[:4], refs[4:]
    copies = field_copies(field_hbm, field, sems)
    start(copies)
    for index in range(TILES):
        wait(copies[index])
        read_field(
            field, index, lambda block, value: put(packed, block, tile(index), value)
        )
    along_lanes(
        lambda index, block: get(packed, block, tile(index)),
        lambda index, block, value: put(packed, block, tile(index), value),
        stage,
        moved,
    )
    deal(info_ref, 0, packed, out_refs)


def column_kernel(info_ref, *refs):
    grad_refs, other_refs, refs = refs[:8], refs[8:16], refs[16:]
    wave_refs, refs = refs[:4], refs[4:]
    onward_refs, (wave, other, stage, held) = refs[: 4 * PIECES], refs[4 * PIECES :]
    use_loss = info_ref[3] == 1
    collect(info_ref, 0, grad_refs, wave)
    along_rows(
        lambda index, block: get(wave, block, tile(index)),
        lambda index, block, value: put(wave, block, tile(index), value),
        stage,
        held,
    )
    deal(info_ref, 1, wave, wave_refs)
    collect(info_ref, 1, other_refs, other)

    def passing(index, block):
        real, imag = get(wave, block, tile(index))
        t_real, t_imag = get(other, block, tile(index))
        return (
            jnp.where(use_loss, t_real, real * t_real + imag * t_imag),
            jnp.where(use_loss, t_imag, imag * t_real - real * t_imag),
        )

    along_rows(
        passing,
        lambda index, block, value: put(other, block, tile(index), value),
        stage,
        held,
    )
    for piece in range(PIECES):
        deal(
            info_ref,
            0,
            other,
            onward_refs[4 * piece : 4 * piece + 4],
            pl.ds(piece * HALF // PIECES, HALF // PIECES),
        )


def write_products(index, wave, lit_x_ref, lit_y_ref, field_ref, out_ref, t_ref, plain_ref):
    lit_y = [
        (lit_y_ref[0, natural(index, half), :], lit_y_ref[1, natural(index, half), :])
        for half in range(2)
    ]
    for pair in range(BLOCKS // 2):
        cols = pl.ds(pair * LANES, LANES)
        left, right = wave(2 * pair), wave(2 * pair + 1)
        reals, imags = halves(left[0], right[0]), halves(left[1], right[1])
        lit_x = (lit_x_ref[0:1, cols], lit_x_ref[1:2, cols])
        for half in range(2):
            rows = natural(index, half)
            real, imag = reals[half], imags[half]
            if t_ref is not None:
                t_real, t_imag = t_ref[0, rows, cols], t_ref[1, rows, cols]
                plain_ref[0, rows, cols] = real * t_real + imag * t_imag
                plain_ref[1, rows, cols] = imag * t_real - real * t_imag
            lit = times(lit_y[half], *lit_x)
            f_real, f_imag = times(lit, field_ref[0, rows, cols], field_ref[1, rows, cols])
            out_ref[0, rows, cols] = real * f_real + imag * f_imag
            out_ref[1, rows, cols] = imag * f_real - real * f_imag


def entry_kernel(info_ref, lit_x_ref, lit_y_ref, field_hbm, *refs):
    wave_refs, (out_hbm, blocks, field, out, in_sems, out_sems) = refs[:8], refs[8:]
    fields = field_copies(field_hbm, field, in_sems)
    outs = field_copies(out, out_hbm, out_sems)
    start(fields)
    collect(info_ref, 1, wave_refs, blocks)
    for index in range(TILES):
        wait(fields[index])
        write_products(
            index,
            lambda block: get(blocks, block, tile(index)),
            lit_x_ref,
            lit_y_ref,
            field,
            out,
            None,
            None,
        )
        start([outs[index]])
    for index in range(TILES):
        wait(outs[index])


def exit_kernel(info_ref, lit_x_ref, lit_y_ref, field_hbm, t_hbm, *refs):
    in_refs, refs = refs[: 8 * PIECES], refs[8 * PIECES :]
    out_hbm, plain_hbm, packed, stage, moved, field, t_field, out, plain, *sems = refs
    fields = field_copies(field_hbm, field, sems[0])
    ts = field_copies(t_hbm, t_field, sems[1])
    outs = field_copies(out, out_hbm, sems[2])
    plains = field_copies(plain, plain_hbm, sems[3])
    for index in range(TILES):
        start([fields[index], ts[index]])
    for piece in range(PIECES):
        collect(
            info_ref,
            0,
            in_refs[8 * piece : 8 * piece + 8],
            packed,
            pl.ds(piece * HALF // PIECES, HALF // PIECES),
        )
    along_lanes(
        lambda index, block: get(packed, block, tile(index)),
        lambda index, block, value: put(packed, block, tile(index), value),
        stage,
        moved,
    )
    for index in range(TILES):
        wait(fields[index] + ts[index])
        write_products(
            index,
            lambda block: get(packed, block, tile(index)),
            lit_x_ref,
            lit_y_ref,
            field,
            out,
            t_field,
            plain,
        )
        start([outs[index], plains[index]])
    for index in range(TILES):
        wait(outs[index] + plains[index])


PIECES = 2
CHAIN = (BLOCKS, 2, HALF, LANES)
BUFFER = pltpu.VMEM(CHAIN, jnp.float32)
HELD = pltpu.VMEM((BLOCKS, 2, 3 * HALF, LANES), jnp.float32)
FIELD = jax.ShapeDtypeStruct((2, WIDTH, N), jnp.float32)
FIELD_BUFFER = pltpu.VMEM(FIELD.shape, jnp.float32)
SEMS = pltpu.SemaphoreType.DMA((TILES, 2, 2))
SPACES = {"s": pltpu.SMEM, "v": pltpu.VMEM, "h": pltpu.HBM}


def groups(pieces=1):
    return (jax.ShapeDtypeStruct((4, 2, 2, HALF // pieces, LANES), jnp.float32),) * 4


def call(kernel, out_shape, out_space, operands, spaces, name, scratch=()):
    outs = jax.tree.leaves(out_shape)
    size = sum(4 * math.prod(x.shape) for x in outs) + sum(4 * x.size for x in operands)
    spaces += "v" * (len(operands) - len(spaces))
    return pl.pallas_call(
        kernel,
        out_shape=out_shape,
        in_specs=[pl.BlockSpec(memory_space=SPACES[space]) for space in spaces],
        out_specs=jax.tree.map(
            lambda _: pl.BlockSpec(memory_space=SPACES[out_space]), out_shape
        ),
        scratch_shapes=list(scratch),
        compiler_params=pltpu.CompilerParams(vmem_limit_bytes=VMEM_LIMIT),
        cost_estimate=pl.CostEstimate(flops=20 * size, bytes_accessed=size, transcendentals=0),
        name=name,
    )(*operands)


def moved_by(order, step, other=0, core=0):
    pairs = []
    for x in range(4):
        for y in range(4):
            near, far = ((x + step) % 4, (y + other) % 4)
            if order == 1:
                near, far = ((x + other) % 4, (y + step) % 4)
            for c in range(2):
                pairs.append((8 * x + 2 * y + c, 8 * near + 2 * far + (c ^ core)))
    return pairs


def send(value, order, step, other=0, core=0, back=False):
    pairs = moved_by(order, step, other, core)
    if back:
        count = lax.axis_size("depth")
        pairs = [
            (BLOCKS * s + i, BLOCKS * ((s - 1) % count) + j)
            for s in range(count)
            for i, j in pairs
        ]
        return lax.ppermute(value, ("depth", "rows"), pairs)
    if step == other == core == 0:
        return value
    return lax.ppermute(value, "rows", pairs)


def exchange(order, dealt, pieces=1, back=False):
    arrived = [send(value, order, step, back=back) for step, value in enumerate(dealt)]
    shape = jax.ShapeDtypeStruct((4, 2, HALF // pieces, LANES), jnp.float32)
    regrouped = call(regroup_kernel, (shape,) * 8, "v", arrived, "", "regroup")
    return [
        send(regrouped[2 * other + core], order, 0, other, core)
        for other in range(4)
        for core in range(2)
    ]


def light(led_number, row_start):
    shift_col = led_number // LED_SIDE - LED_SIDE // 2
    shift_row = led_number % LED_SIDE - LED_SIDE // 2
    cols = shift_col * jnp.arange(N, dtype=jnp.int32) % N
    rows = shift_row * (row_start + jnp.arange(WIDTH, dtype=jnp.int32)) % N
    angle_x = 2.0 * math.pi / N * cols.astype(jnp.float32)
    angle_y = 2.0 * math.pi / N * rows.astype(jnp.float32)
    lit_x = jnp.stack([jnp.cos(angle_x), jnp.sin(angle_x)])
    lit_y = jnp.stack([jnp.cos(angle_y), jnp.sin(angle_y)])
    return lit_x, jnp.broadcast_to(lit_y[:, :, None], (2, WIDTH, LANES))


def per_device(grad_arriving, loss_grad, t_entry, t_exit, fields_entry, fields_exit, led_index):
    place = lax.axis_index("rows")
    first = (lax.axis_index("depth") == 0).astype(jnp.int32)
    info = jnp.stack([place // 8, place // 2 % 4, place % 2, first]).astype(jnp.int32)
    dealt_other = call(
        other_kernel,
        groups(),
        "v",
        [info, t_entry[0], loss_grad],
        "shh",
        "other",
        [FIELD_BUFFER, BUFFER, SEMS],
    )
    other = exchange(1, dealt_other)
    dealt_grad = call(
        enter_kernel,
        groups(),
        "v",
        [info, grad_arriving[0]],
        "sh",
        "enter",
        [FIELD_BUFFER, BUFFER, BUFFER, BUFFER, SEMS],
    )
    grad = exchange(0, dealt_grad)
    dealt = call(
        column_kernel,
        groups() + groups(PIECES) * PIECES,
        "v",
        [info, *grad, *other],
        "s",
        "columns",
        [BUFFER, BUFFER, BUFFER, HELD],
    )
    arrived = []
    for piece in range(PIECES):
        arrived += exchange(0, dealt[4 + 4 * piece : 8 + 4 * piece], PIECES, back=True)
    wave = exchange(1, dealt[:4])
    grad_entry = call(
        entry_kernel,
        FIELD,
        "h",
        [info, *light(led_index[0, 0], place * WIDTH), fields_entry[0], *wave],
        "svvh",
        "entry",
        [BUFFER, FIELD_BUFFER, FIELD_BUFFER, SEMS, SEMS],
    )
    grad_exit, leaving = call(
        exit_kernel,
        (FIELD, FIELD),
        "h",
        [info, *light(led_index[0, 1], place * WIDTH), fields_exit[0], t_exit[0], *arrived],
        "svvhh",
        "exit",
        [BUFFER, BUFFER, BUFFER] + [FIELD_BUFFER] * 4 + [SEMS] * 4,
    )
    return (grad_entry[None], grad_exit[None], leaving[None])


def solution(mesh):
    spread = P("depth", None, "rows", None)
    return jax.shard_map(
        per_device,
        mesh=mesh,
        in_specs=(spread, P(None, "rows", None), spread, spread, spread, spread, P("depth", None)),
        out_specs=(spread, spread, spread),
        check_vma=False,
    )
```

```python
import functools
import math

import jax
import jax.numpy as jnp
import numpy as np
from jax import lax
from jax.experimental import pallas as pl
from jax.experimental.pallas import tpu as pltpu
from jax.sharding import PartitionSpec as P

LED_SIDE = 15
SPREAD = 3
BLOCKS = 32
N = 2048
WIDTH = N // BLOCKS
LANES = 2 * WIDTH
HALF = WIDTH // 2
TILES = HALF // 8
VMEM_LIMIT = 24 * 1024 * 1024

INVERSE = pow(SPREAD, -1, N)
_k = np.arange(N, dtype=np.int64)
GAUSS = np.exp(-2j * np.pi * ((SPREAD * _k * _k) % N) / N).sum() / N


def chirp_gain(distance):
    return complex(GAUSS * np.exp(2j * np.pi * ((INVERSE * distance * distance) % N) / N))


def shift_of(freq):
    pairs = SPREAD * (freq - BLOCKS // 2) % BLOCKS
    return 2 * pairs, chirp_gain(-pairs), chirp_gain(BLOCKS - pairs)


def plus(a, b):
    return (a[0] + b[0], a[1] + b[1])


def minus(a, b):
    return (a[0] - b[0], a[1] - b[1])


def times_i(a):
    return (-a[1], a[0])


def times(a, real, imag):
    return (a[0] * real - a[1] * imag, a[0] * imag + a[1] * real)


def scaled(a, factor):
    return times(a, np.float32(factor.real), np.float32(factor.imag))


def turned(a, step, count, sign):
    step = step * sign % count
    if step == 0:
        return a
    if 2 * step == count:
        return (-a[0], -a[1])
    if 4 * step == count:
        return times_i(a)
    if 4 * step == 3 * count:
        return (a[1], -a[0])
    if 8 * step % count == 0:
        root = np.float32(math.sqrt(0.5))
        eighth = 8 * step // count
        added, taken = (a[0] + a[1]) * root, (a[0] - a[1]) * root
        return {
            1: (taken, added),
            3: (-added, taken),
            5: (-taken, -added),
            7: (added, -taken),
        }[eighth]
    angle = 2.0 * math.pi * step / count
    return scaled(a, complex(math.cos(angle), math.sin(angle)))


def small_dft(values, sign):
    count = len(values)
    if count == 1:
        return values
    if count == 2:
        return [plus(*values), minus(*values)]
    quarter = count // 4
    parts = [small_dft(values[phase::4], sign) for phase in range(4)]
    result = [None] * count
    for j in range(quarter):
        a, b, c, d = (turned(parts[k][j], j * k, count, sign) for k in range(4))
        sum_ac, dif_ac, sum_bd, dif_bd = plus(a, c), minus(a, c), plus(b, d), minus(b, d)
        result[j] = plus(sum_ac, sum_bd)
        result[j + 2 * quarter] = minus(sum_ac, sum_bd)
        up = (dif_ac[0] - dif_bd[1], dif_ac[1] + dif_bd[0])
        down = (dif_ac[0] + dif_bd[1], dif_ac[1] - dif_bd[0])
        result[j + quarter], result[j + 3 * quarter] = (up, down) if sign > 0 else (down, up)
    return result


def lane_ids():
    return lax.broadcasted_iota(jnp.int32, (8, LANES), 1)


def halves(first, second):
    low = lane_ids() < WIDTH
    return (
        jnp.where(low, first, pltpu.roll(second, WIDTH, 1)),
        jnp.where(low, pltpu.roll(first, WIDTH, 1), second),
    )


def tile(index):
    return pl.ds(8 * index, 8)


def get(ref, block, rows):
    return (ref[block, 0, rows, :], ref[block, 1, rows, :])


def put(ref, block, rows, value):
    ref[block, 0, rows, :] = value[0]
    ref[block, 1, rows, :] = value[1]


def block_dft(load, emit, stage, rows, sign):
    for k in range(4):
        for j, value in enumerate(small_dft([load(4 * n + k) for n in range(8)], sign)):
            put(stage, 8 * k + j, rows, turned(value, j * k, BLOCKS, sign))
    for j in range(8):
        outs = small_dft([get(stage, 8 * k + j, rows) for k in range(4)], sign)
        for step, value in enumerate(outs):
            emit(j + 8 * step, value)


def along_lanes(index, source, target, stage, moved, place=None):
    inside = lane_ids() % WIDTH
    rows = tile(index)
    source_rows = rows if place is None else tile(place)

    def move(freq, value):
        shift, plain, wrapped = shift_of(freq)
        if shift:
            mask = inside >= shift
            value = tuple(
                jnp.where(mask, pltpu.roll(v, shift, 1), pltpu.roll(v, shift + WIDTH, 1))
                for v in value
            )
            real = jnp.where(mask, np.float32(plain.real), np.float32(wrapped.real))
            imag = jnp.where(mask, np.float32(plain.imag), np.float32(wrapped.imag))
            value = times(value, real, imag)
        else:
            value = scaled(value, plain)
        put(moved, freq, rows, value)

    block_dft(lambda block: get(source, block, source_rows), move, stage, rows, -1)
    block_dft(
        lambda freq: get(moved, freq, rows),
        lambda block, value: put(target, block, rows, value),
        stage,
        rows,
        1,
    )


def along_rows(load, store, stage, held):
    low = lane_ids() < WIDTH
    for index in range(TILES):
        rows = tile(index)

        def hold(freq, value):
            shift, plain, wrapped = shift_of(freq)
            plain = scaled(value, plain)
            wrapped = scaled(value, wrapped) if shift else None
            if shift > HALF:
                put(held, freq, rows, wrapped)
            if shift < HALF:
                put(held, freq, pl.ds(2 * HALF + 8 * index, 8), plain)
            if shift:
                crossed = tuple(
                    pltpu.roll(jnp.where(low, p, w), WIDTH, 1) for p, w in zip(plain, wrapped)
                )
                put(held, freq, pl.ds(HALF + 8 * index, 8), crossed)

        block_dft(functools.partial(load, index), hold, stage, rows, -1)
    for index in range(TILES):
        block_dft(
            lambda freq: get(held, freq, pl.ds(2 * HALF - shift_of(freq)[0] + 8 * index, 8)),
            functools.partial(store, index),
            stage,
            tile(index),
            1,
        )


def natural(index, half):
    return pl.ds(8 * index + HALF * half, 8)


def field_copies(source, target, sems):
    return [
        [
            pltpu.make_async_copy(
                source.at[part, natural(index, half), :],
                target.at[part, natural(index, half), :],
                sems.at[index, part, half],
            )
            for part in range(2)
            for half in range(2)
        ]
        for index in range(TILES)
    ]


def start(copies):
    for tile_copies in copies:
        for copy in tile_copies:
            copy.start()


def wait(tile_copies):
    for copy in tile_copies:
        copy.wait()


def read_field(ref, index, write):
    for pair in range(BLOCKS // 2):
        cols = pl.ds(pair * LANES, LANES)
        parts = [
            halves(ref[part, natural(index, 0), cols], ref[part, natural(index, 1), cols])
            for part in range(2)
        ]
        for side in range(2):
            write(2 * pair + side, (parts[0][side], parts[1][side]))


def enter_kernel(first_ref, field_hbm, t_hbm, loss_hbm, out_ref, field, other, stage, moved, *sems):
    use_loss = first_ref[0] == 1
    fields = field_copies(field_hbm, field, sems[0])
    from_loss, from_t = (field_copies(hbm, other, sems[1]) for hbm in (loss_hbm, t_hbm))
    start(fields)

    @pl.when(use_loss)
    def _():
        start(from_loss)

    @pl.when(jnp.logical_not(use_loss))
    def _():
        start(from_t)

    grad_out, other_out = out_ref.at[:, 0], out_ref.at[:, 1]
    for index in range(TILES):
        wait(fields[index])
        read_field(
            field, index, lambda block, value: put(grad_out, block, tile(index), value)
        )
        along_lanes(index, grad_out, grad_out, stage, moved)
    for index in range(TILES):
        wait(from_t[index])
        read_field(
            other, index, lambda block, value: put(other_out, block, tile(index), value)
        )


def column_kernel(first_ref, in_ref, early_ref, late_ref, stage, held):
    use_loss = first_ref[0] == 1

    def put_wave(index, block, value):
        put(early_ref, block, tile(index), value)

    def put_onward(index, block, value):
        if index < EARLY:
            put(early_ref, block, tile(TILES + index), value)
        else:
            put(late_ref, block, tile(index - EARLY), value)

    def passing(index, block):
        real, imag = get(early_ref, block, tile(index))
        t_real, t_imag = get(in_ref.at[:, 1], block, tile(index))
        return (
            jnp.where(use_loss, t_real, real * t_real + imag * t_imag),
            jnp.where(use_loss, t_imag, imag * t_real - real * t_imag),
        )

    along_rows(
        lambda index, block: get(in_ref.at[:, 0], block, tile(index)), put_wave, stage, held
    )
    along_rows(passing, put_onward, stage, held)


def write_products(index, wave, lit_x_ref, lit_y_ref, field_ref, out_ref, t_ref, plain_ref):
    lit_y = [
        (lit_y_ref[0, natural(index, half), :], lit_y_ref[1, natural(index, half), :])
        for half in range(2)
    ]
    for pair in range(BLOCKS // 2):
        cols = pl.ds(pair * LANES, LANES)
        left, right = wave(2 * pair), wave(2 * pair + 1)
        reals, imags = halves(left[0], right[0]), halves(left[1], right[1])
        lit_x = (lit_x_ref[0:1, cols], lit_x_ref[1:2, cols])
        for half in range(2):
            rows = natural(index, half)
            real, imag = reals[half], imags[half]
            if t_ref is not None:
                t_real, t_imag = t_ref[0, rows, cols], t_ref[1, rows, cols]
                plain_ref[0, rows, cols] = real * t_real + imag * t_imag
                plain_ref[1, rows, cols] = imag * t_real - real * t_imag
            lit = times(lit_y[half], *lit_x)
            f_real, f_imag = times(lit, field_ref[0, rows, cols], field_ref[1, rows, cols])
            out_ref[0, rows, cols] = real * f_real + imag * f_imag
            out_ref[1, rows, cols] = imag * f_real - real * f_imag


def entry_kernel(lit_x_ref, lit_y_ref, field_hbm, wave_ref, out_hbm, field, out, *sems):
    fields = field_copies(field_hbm, field, sems[0])
    outs = field_copies(out, out_hbm, sems[1])
    start(fields)
    for index in range(TILES):
        wait(fields[index])
        write_products(
            index,
            lambda block: get(wave_ref, block, tile(index)),
            lit_x_ref,
            lit_y_ref,
            field,
            out,
            None,
            None,
        )
        start([outs[index]])
    for index in range(TILES):
        wait(outs[index])


def exit_kernel(lit_x_ref, lit_y_ref, field_hbm, t_hbm, early_ref, late_ref, *refs):
    out_hbm, plain_hbm, packed, stage, moved, field, t_field, out, plain, *sems = refs
    fields = field_copies(field_hbm, field, sems[0])
    ts = field_copies(t_hbm, t_field, sems[1])
    outs = field_copies(out, out_hbm, sems[2])
    plains = field_copies(plain, plain_hbm, sems[3])
    for index in range(TILES):
        start([fields[index], ts[index]])
    for index in range(TILES):
        source, place = (early_ref, index) if index < EARLY else (late_ref, index - EARLY)
        along_lanes(index, source, packed, stage, moved, place)
        wait(fields[index] + ts[index])
        write_products(
            index,
            lambda block: get(packed, block, tile(index)),
            lit_x_ref,
            lit_y_ref,
            field,
            out,
            t_field,
            plain,
        )
        start([outs[index], plains[index]])
    for index in range(TILES):
        wait(outs[index] + plains[index])


EARLY = 1
CHAIN = (BLOCKS, 2, HALF, LANES)
BUFFER = pltpu.VMEM(CHAIN, jnp.float32)
HELD = pltpu.VMEM((BLOCKS, 2, 3 * HALF, LANES), jnp.float32)
BOTH = jax.ShapeDtypeStruct((BLOCKS, 2, 2, HALF, LANES), jnp.float32)
SECOND = jax.ShapeDtypeStruct((BLOCKS, 2, HALF + 8 * EARLY, LANES), jnp.float32)
THIRD = jax.ShapeDtypeStruct((BLOCKS, 2, HALF - 8 * EARLY, LANES), jnp.float32)
FIELD = jax.ShapeDtypeStruct((2, WIDTH, N), jnp.float32)
FIELD_BUFFER = pltpu.VMEM(FIELD.shape, jnp.float32)
SEMS = pltpu.SemaphoreType.DMA((TILES, 2, 2))
SPACES = {"s": pltpu.SMEM, "v": pltpu.VMEM, "h": pltpu.HBM}


def call(kernel, out_shape, out_space, operands, spaces, name, scratch=()):
    outs = jax.tree.leaves(out_shape)
    size = sum(4 * math.prod(x.shape) for x in outs) + sum(4 * x.size for x in operands)
    spaces += "v" * (len(operands) - len(spaces))
    return pl.pallas_call(
        kernel,
        out_shape=out_shape,
        in_specs=[pl.BlockSpec(memory_space=SPACES[space]) for space in spaces],
        out_specs=jax.tree.map(
            lambda _: pl.BlockSpec(memory_space=SPACES[out_space]), out_shape
        ),
        scratch_shapes=list(scratch),
        compiler_params=pltpu.CompilerParams(vmem_limit_bytes=VMEM_LIMIT),
        cost_estimate=pl.CostEstimate(flops=20 * size, bytes_accessed=size, transcendentals=0),
        name=name,
    )(*operands)


def exchange(packed):
    return lax.all_to_all(packed, "rows", split_axis=0, concat_axis=0, tiled=True)


def to_previous(value):
    count = lax.axis_size("depth")
    return lax.ppermute(value, "depth", [(s, (s - 1) % count) for s in range(count)])


def light(led_number, row_start):
    shift_col = led_number // LED_SIDE - LED_SIDE // 2
    shift_row = led_number % LED_SIDE - LED_SIDE // 2
    cols = shift_col * jnp.arange(N, dtype=jnp.int32) % N
    rows = shift_row * (row_start + jnp.arange(WIDTH, dtype=jnp.int32)) % N
    angle_x = 2.0 * math.pi / N * cols.astype(jnp.float32)
    angle_y = 2.0 * math.pi / N * rows.astype(jnp.float32)
    lit_x = jnp.stack([jnp.cos(angle_x), jnp.sin(angle_x)])
    lit_y = jnp.stack([jnp.cos(angle_y), jnp.sin(angle_y)])
    return lit_x, jnp.broadcast_to(lit_y[:, :, None], (2, WIDTH, LANES))


def per_device(grad_arriving, loss_grad, t_entry, t_exit, fields_entry, fields_exit, led_index):
    row_start = lax.axis_index("rows") * WIDTH
    first = (lax.axis_index("depth") == 0).astype(jnp.int32).reshape(1)
    both = call(
        enter_kernel,
        BOTH,
        "v",
        [first, grad_arriving[0], t_entry[0], loss_grad],
        "shhh",
        "enter",
        [FIELD_BUFFER, FIELD_BUFFER, BUFFER, BUFFER, SEMS, SEMS],
    )
    early, late = call(
        column_kernel,
        (SECOND, THIRD),
        "v",
        [first, exchange(both)],
        "s",
        "columns",
        [BUFFER, HELD],
    )
    late = to_previous(late)
    early = exchange(early)
    grad_entry = call(
        entry_kernel,
        FIELD,
        "h",
        [*light(led_index[0, 0], row_start), fields_entry[0], early],
        "vvh",
        "entry",
        [FIELD_BUFFER, FIELD_BUFFER, SEMS, SEMS],
    )
    grad_exit, leaving = call(
        exit_kernel,
        (FIELD, FIELD),
        "h",
        [
            *light(led_index[0, 1], row_start),
            fields_exit[0],
            t_exit[0],
            to_previous(early[:, :, HALF:, :]),
            exchange(late),
        ],
        "vvhh",
        "exit",
        [BUFFER, BUFFER, BUFFER] + [FIELD_BUFFER] * 4 + [SEMS] * 4,
    )
    return (grad_entry[None], grad_exit[None], leaving[None])


def solution(mesh):
    spread = P("depth", None, "rows", None)
    return jax.shard_map(
        per_device,
        mesh=mesh,
        in_specs=(spread, P(None, "rows", None), spread, spread, spread, spread, P("depth", None)),
        out_specs=(spread, spread, spread),
        check_vma=False,
    )
```

```python
import functools
import math

import jax
import jax.numpy as jnp
import numpy as np
from jax import lax
from jax.experimental import pallas as pl
from jax.experimental.pallas import tpu as pltpu
from jax.sharding import PartitionSpec as P

LED_SIDE = 15
SPREAD = 3
BLOCKS = 32
N = 2048
WIDTH = N // BLOCKS
LANES = 2 * WIDTH
HALF = WIDTH // 2
TILES = HALF // 8
VMEM_LIMIT = 16 * 1024 * 1024

INVERSE = pow(SPREAD, -1, N)
_k = np.arange(N, dtype=np.int64)
GAUSS = np.exp(-2j * np.pi * ((SPREAD * _k * _k) % N) / N).sum() / N


def chirp_gain(distance):
    return complex(GAUSS * np.exp(2j * np.pi * ((INVERSE * distance * distance) % N) / N))


def shift_of(freq):
    pairs = SPREAD * (freq - BLOCKS // 2) % BLOCKS
    return 2 * pairs, chirp_gain(-pairs), chirp_gain(BLOCKS - pairs)


def plus(a, b):
    return (a[0] + b[0], a[1] + b[1])


def minus(a, b):
    return (a[0] - b[0], a[1] - b[1])


def times_i(a):
    return (-a[1], a[0])


def times(a, real, imag):
    return (a[0] * real - a[1] * imag, a[0] * imag + a[1] * real)


def scaled(a, factor):
    return times(a, np.float32(factor.real), np.float32(factor.imag))


def turned(a, step, count, sign):
    step = step * sign % count
    if step == 0:
        return a
    if 2 * step == count:
        return (-a[0], -a[1])
    if 4 * step == count:
        return times_i(a)
    if 4 * step == 3 * count:
        return (a[1], -a[0])
    if 8 * step % count == 0:
        root = np.float32(math.sqrt(0.5))
        eighth = 8 * step // count
        added, taken = (a[0] + a[1]) * root, (a[0] - a[1]) * root
        return {
            1: (taken, added),
            3: (-added, taken),
            5: (-taken, -added),
            7: (added, -taken),
        }[eighth]
    angle = 2.0 * math.pi * step / count
    return scaled(a, complex(math.cos(angle), math.sin(angle)))


def small_dft(values, sign):
    count = len(values)
    if count == 1:
        return values
    if count == 2:
        return [plus(*values), minus(*values)]
    quarter = count // 4
    parts = [small_dft(values[phase::4], sign) for phase in range(4)]
    result = [None] * count
    for j in range(quarter):
        a, b, c, d = (turned(parts[k][j], j * k, count, sign) for k in range(4))
        sum_ac, dif_ac, sum_bd, dif_bd = plus(a, c), minus(a, c), plus(b, d), minus(b, d)
        result[j] = plus(sum_ac, sum_bd)
        result[j + 2 * quarter] = minus(sum_ac, sum_bd)
        up = (dif_ac[0] - dif_bd[1], dif_ac[1] + dif_bd[0])
        down = (dif_ac[0] + dif_bd[1], dif_ac[1] - dif_bd[0])
        result[j + quarter], result[j + 3 * quarter] = (up, down) if sign > 0 else (down, up)
    return result


def lane_ids():
    return lax.broadcasted_iota(jnp.int32, (8, LANES), 1)


def halves(first, second):
    low = lane_ids() < WIDTH
    return (
        jnp.where(low, first, pltpu.roll(second, WIDTH, 1)),
        jnp.where(low, pltpu.roll(first, WIDTH, 1), second),
    )


def tile(index):
    return pl.ds(8 * index, 8)


def get(ref, block, rows):
    return (ref[block, 0, rows, :], ref[block, 1, rows, :])


def put(ref, block, rows, value):
    ref[block, 0, rows, :] = value[0]
    ref[block, 1, rows, :] = value[1]


def block_dft(load, emit, stage, rows, sign):
    for k in range(4):
        for j, value in enumerate(small_dft([load(4 * n + k) for n in range(8)], sign)):
            put(stage, 8 * k + j, rows, turned(value, j * k, BLOCKS, sign))
    for j in range(8):
        outs = small_dft([get(stage, 8 * k + j, rows) for k in range(4)], sign)
        for step, value in enumerate(outs):
            emit(j + 8 * step, value)


def along_lanes(load, store, stage, moved):
    inside = lane_ids() % WIDTH
    for index in range(TILES):
        rows = tile(index)

        def move(freq, value):
            shift, plain, wrapped = shift_of(freq)
            if shift:
                mask = inside >= shift
                value = tuple(
                    jnp.where(mask, pltpu.roll(v, shift, 1), pltpu.roll(v, shift + WIDTH, 1))
                    for v in value
                )
                real = jnp.where(mask, np.float32(plain.real), np.float32(wrapped.real))
                imag = jnp.where(mask, np.float32(plain.imag), np.float32(wrapped.imag))
                value = times(value, real, imag)
            else:
                value = scaled(value, plain)
            put(moved, freq, rows, value)

        block_dft(functools.partial(load, index), move, stage, rows, -1)
        block_dft(
            lambda freq: get(moved, freq, rows), functools.partial(store, index), stage, rows, 1
        )


def along_rows(load, store, stage, held):
    low = lane_ids() < WIDTH
    for index in range(TILES):
        rows = tile(index)

        def hold(freq, value):
            shift, plain, wrapped = shift_of(freq)
            plain = scaled(value, plain)
            wrapped = scaled(value, wrapped) if shift else None
            if shift > HALF:
                put(held, freq, rows, wrapped)
            if shift < HALF:
                put(held, freq, pl.ds(2 * HALF + 8 * index, 8), plain)
            if shift:
                crossed = tuple(
                    pltpu.roll(jnp.where(low, p, w), WIDTH, 1) for p, w in zip(plain, wrapped)
                )
                put(held, freq, pl.ds(HALF + 8 * index, 8), crossed)

        block_dft(functools.partial(load, index), hold, stage, rows, -1)
    for index in range(TILES):
        block_dft(
            lambda freq: get(held, freq, pl.ds(2 * HALF - shift_of(freq)[0] + 8 * index, 8)),
            functools.partial(store, index),
            stage,
            tile(index),
            1,
        )


def natural(index, half):
    return pl.ds(8 * index + HALF * half, 8)


def read_pair(ref, index, pair):
    cols = pl.ds(pair * LANES, LANES)
    parts = [
        halves(ref[part, natural(index, 0), cols], ref[part, natural(index, 1), cols])
        for part in range(2)
    ]
    return [(parts[0][side], parts[1][side]) for side in range(2)]


def read_field(ref, write):
    for index in range(TILES):
        for pair in range(BLOCKS // 2):
            for side, value in enumerate(read_pair(ref, index, pair)):
                write(index, 2 * pair + side, value)


def enter_kernel(field_ref, other_ref, out_ref, packed, stage, moved):
    read_field(field_ref, lambda index, block, value: put(packed, block, tile(index), value))
    along_lanes(
        lambda index, block: get(packed, block, tile(index)),
        lambda index, block, value: put(out_ref.at[:, 0], block, tile(index), value),
        stage,
        moved,
    )
    read_field(
        other_ref, lambda index, block, value: put(out_ref.at[:, 1], block, tile(index), value)
    )


def column_kernel(info_ref, in_ref, wave_ref, out_ref, stage, held):
    use_loss = info_ref[1] == 1
    along_rows(
        lambda index, block: get(in_ref.at[:, 0], block, tile(index)),
        lambda index, block, value: put(wave_ref, block, tile(index), value),
        stage,
        held,
    )

    def passing(index, block):
        real, imag = get(wave_ref, block, tile(index))
        t_real, t_imag = get(in_ref.at[:, 1], block, tile(index))
        return (
            jnp.where(use_loss, t_real, real * t_real + imag * t_imag),
            jnp.where(use_loss, t_imag, imag * t_real - real * t_imag),
        )

    along_rows(
        passing,
        lambda index, block, value: put(out_ref, block, tile(index), value),
        stage,
        held,
    )


def light_tables():
    shifts = np.arange(LED_SIDE) - LED_SIDE // 2
    along_x = np.exp(2j * np.pi * (shifts[:, None] * np.arange(N) % N) / N)
    along_y = np.zeros((WIDTH, LANES), np.complex128)
    along_y[:, :LED_SIDE] = np.exp(2j * np.pi * (np.arange(WIDTH)[:, None] * shifts % N) / N)
    turns = np.exp(2j * np.pi * np.arange(BLOCKS) / BLOCKS)
    return (
        np.concatenate([along_x.real, along_x.imag]).reshape(-1, N // LANES, LANES).astype(np.float32),
        np.stack([along_y.real, along_y.imag]).astype(np.float32),
        np.stack([turns.real, turns.imag]).astype(np.float32),
    )


def write_products(
    tick, led_ref, info_ref, turn_ref, lit_x_ref, lit_y_ref, wave, field_ref, out_ref, *plain
):
    led = led_ref[0, tick]
    column_shift = led // LED_SIDE
    row_shift = led - column_shift * LED_SIDE
    turn = (info_ref[0] * (row_shift - LED_SIDE // 2)) & (BLOCKS - 1)
    turn_real, turn_imag = turn_ref[0, turn], turn_ref[1, turn]
    chosen = lane_ids() == row_shift

    def lit_rows(rows):
        pair = tuple(
            jnp.sum(jnp.where(chosen, lit_y_ref[part, rows, :], 0.0), axis=1, keepdims=True)
            for part in range(2)
        )
        pair = tuple(jnp.broadcast_to(v, (8, LANES)) for v in pair)
        return times(pair, turn_real, turn_imag)

    for index in range(TILES):
        lit_y = [lit_rows(natural(index, half)) for half in range(2)]
        for pair in range(BLOCKS // 2):
            cols = pl.ds(pair * LANES, LANES)
            left, right = wave(index, 2 * pair), wave(index, 2 * pair + 1)
            reals, imags = halves(left[0], right[0]), halves(left[1], right[1])
            lit_x = (
                lit_x_ref[column_shift, pair : pair + 1, :],
                lit_x_ref[column_shift + LED_SIDE, pair : pair + 1, :],
            )
            for half in range(2):
                rows = natural(index, half)
                real, imag = reals[half], imags[half]
                if plain:
                    t_ref, plain_ref = plain
                    t_real, t_imag = t_ref[0, rows, cols], t_ref[1, rows, cols]
                    plain_ref[0, rows, cols] = real * t_real + imag * t_imag
                    plain_ref[1, rows, cols] = imag * t_real - real * t_imag
                lit = times(lit_y[half], *lit_x)
                f_real, f_imag = times(lit, field_ref[0, rows, cols], field_ref[1, rows, cols])
                out_ref[0, rows, cols] = real * f_real + imag * f_imag
                out_ref[1, rows, cols] = imag * f_real - real * f_imag


def entry_kernel(led_ref, info_ref, turn_ref, lit_x_ref, lit_y_ref, field_ref, wave_ref, out_ref):
    write_products(
        0,
        led_ref,
        info_ref,
        turn_ref,
        lit_x_ref,
        lit_y_ref,
        lambda index, block: get(wave_ref, block, tile(index)),
        field_ref,
        out_ref,
    )


def exit_kernel(
    led_ref,
    info_ref,
    turn_ref,
    lit_x_ref,
    lit_y_ref,
    field_ref,
    t_ref,
    in_ref,
    out_ref,
    plain_ref,
    packed,
    stage,
    moved,
):
    along_lanes(
        lambda index, block: get(in_ref, block, tile(index)),
        lambda index, block, value: put(packed, block, tile(index), value),
        stage,
        moved,
    )
    write_products(
        1,
        led_ref,
        info_ref,
        turn_ref,
        lit_x_ref,
        lit_y_ref,
        lambda index, block: get(packed, block, tile(index)),
        field_ref,
        out_ref,
        t_ref,
        plain_ref,
    )


WHOLE = pl.BlockSpec(memory_space=pltpu.VMEM)
SCALAR = pl.BlockSpec(memory_space=pltpu.SMEM)
CHAIN = (BLOCKS, 2, HALF, LANES)
PACKED = jax.ShapeDtypeStruct(CHAIN, jnp.float32)
BOTH = jax.ShapeDtypeStruct((BLOCKS, 2, 2, HALF, LANES), jnp.float32)
FIELD = jax.ShapeDtypeStruct((2, WIDTH, N), jnp.float32)
BUFFER = pltpu.VMEM(CHAIN, jnp.float32)
HELD = pltpu.VMEM((BLOCKS, 2, 3 * HALF, LANES), jnp.float32)


def call(kernel, out_shape, operands, name, scratch=(), scalars=0):
    outs = jax.tree.leaves(out_shape)
    size = sum(4 * math.prod(x.shape) for x in outs) + sum(4 * x.size for x in operands)
    return pl.pallas_call(
        kernel,
        out_shape=out_shape,
        in_specs=[SCALAR] * scalars + [WHOLE] * (len(operands) - scalars),
        out_specs=jax.tree.map(lambda _: WHOLE, out_shape),
        scratch_shapes=list(scratch),
        compiler_params=pltpu.CompilerParams(vmem_limit_bytes=VMEM_LIMIT),
        cost_estimate=pl.CostEstimate(flops=20 * size, bytes_accessed=size, transcendentals=0),
        name=name,
    )(*operands)


def exchange(packed):
    return lax.all_to_all(packed, "rows", split_axis=0, concat_axis=0, tiled=True)


def to_previous(value):
    count = lax.axis_size("depth")
    return lax.ppermute(value, "depth", [(s, (s - 1) % count) for s in range(count)])


def per_device(grad_arriving, loss_grad, t_entry, t_exit, fields_entry, fields_exit, led_index):
    first = (lax.axis_index("depth") == 0).astype(jnp.int32)
    info = jnp.stack([lax.axis_index("rows"), first]).astype(jnp.int32)
    lit_x, lit_y, turns = (jnp.asarray(table) for table in light_tables())
    lights = [led_index, info, turns, lit_x, lit_y]
    both = call(
        enter_kernel,
        BOTH,
        [grad_arriving[0], jnp.where(first == 1, loss_grad, t_entry[0])],
        "enter",
        [BUFFER, BUFFER, BUFFER],
    )
    wave, onward = call(
        column_kernel, (PACKED, PACKED), [info, exchange(both)], "columns", [BUFFER, HELD], 1
    )
    onward = to_previous(onward)
    wave = exchange(wave)
    grad_entry = call(entry_kernel, FIELD, [*lights, fields_entry[0], wave], "entry", scalars=3)
    onward, grad_entry = lax.optimization_barrier((onward, grad_entry))
    grad_exit, leaving = call(
        exit_kernel,
        (FIELD, FIELD),
        [*lights, fields_exit[0], t_exit[0], exchange(onward)],
        "exit",
        [BUFFER, BUFFER, BUFFER],
        3,
    )
    return (grad_entry[None], grad_exit[None], leaving[None])


def solution(mesh):
    spread = P("depth", None, "rows", None)
    return jax.shard_map(
        per_device,
        mesh=mesh,
        in_specs=(spread, P(None, "rows", None), spread, spread, spread, spread, P("depth", None)),
        out_specs=(spread, spread, spread),
        check_vma=False,
    )
```

```python
import functools
import math

import jax
import jax.numpy as jnp
import numpy as np
from jax import lax
from jax.experimental import pallas as pl
from jax.experimental.pallas import tpu as pltpu
from jax.sharding import PartitionSpec as P

LED_SIDE = 15
SPREAD = 3
BLOCKS = 32
N = 2048
WIDTH = N // BLOCKS
LANES = 2 * WIDTH
HALF = WIDTH // 2
TILES = HALF // 8
VMEM_LIMIT = 16 * 1024 * 1024

INVERSE = pow(SPREAD, -1, N)
_k = np.arange(N, dtype=np.int64)
GAUSS = np.exp(-2j * np.pi * ((SPREAD * _k * _k) % N) / N).sum() / N


def chirp_gain(distance):
    return complex(GAUSS * np.exp(2j * np.pi * ((INVERSE * distance * distance) % N) / N))


def shift_of(freq):
    pairs = SPREAD * (freq - BLOCKS // 2) % BLOCKS
    return 2 * pairs, chirp_gain(-pairs), chirp_gain(BLOCKS - pairs)


def plus(a, b):
    return (a[0] + b[0], a[1] + b[1])


def minus(a, b):
    return (a[0] - b[0], a[1] - b[1])


def times_i(a):
    return (-a[1], a[0])


def times(a, real, imag):
    return (a[0] * real - a[1] * imag, a[0] * imag + a[1] * real)


def scaled(a, factor):
    return times(a, np.float32(factor.real), np.float32(factor.imag))


def turned(a, step, count, sign):
    step = step * sign % count
    if step == 0:
        return a
    if 2 * step == count:
        return (-a[0], -a[1])
    if 4 * step == count:
        return times_i(a)
    if 4 * step == 3 * count:
        return (a[1], -a[0])
    if 8 * step % count == 0:
        root = np.float32(math.sqrt(0.5))
        eighth = 8 * step // count
        added, taken = (a[0] + a[1]) * root, (a[0] - a[1]) * root
        return {
            1: (taken, added),
            3: (-added, taken),
            5: (-taken, -added),
            7: (added, -taken),
        }[eighth]
    angle = 2.0 * math.pi * step / count
    return scaled(a, complex(math.cos(angle), math.sin(angle)))


def small_dft(values, sign):
    count = len(values)
    if count == 1:
        return values
    if count == 2:
        return [plus(*values), minus(*values)]
    quarter = count // 4
    parts = [small_dft(values[phase::4], sign) for phase in range(4)]
    result = [None] * count
    for j in range(quarter):
        a, b, c, d = (turned(parts[k][j], j * k, count, sign) for k in range(4))
        sum_ac, dif_ac, sum_bd, dif_bd = plus(a, c), minus(a, c), plus(b, d), minus(b, d)
        result[j] = plus(sum_ac, sum_bd)
        result[j + 2 * quarter] = minus(sum_ac, sum_bd)
        up = (dif_ac[0] - dif_bd[1], dif_ac[1] + dif_bd[0])
        down = (dif_ac[0] + dif_bd[1], dif_ac[1] - dif_bd[0])
        result[j + quarter], result[j + 3 * quarter] = (up, down) if sign > 0 else (down, up)
    return result


def lane_ids():
    return lax.broadcasted_iota(jnp.int32, (8, LANES), 1)


def halves(first, second):
    low = lane_ids() < WIDTH
    return (
        jnp.where(low, first, pltpu.roll(second, WIDTH, 1)),
        jnp.where(low, pltpu.roll(first, WIDTH, 1), second),
    )


def tile(index):
    return pl.ds(8 * index, 8)


def get(ref, block, rows):
    return (ref[block, 0, rows, :], ref[block, 1, rows, :])


def put(ref, block, rows, value):
    ref[block, 0, rows, :] = value[0]
    ref[block, 1, rows, :] = value[1]


def block_dft(load, emit, stage, rows, sign):
    for k in range(4):
        for j, value in enumerate(small_dft([load(4 * n + k) for n in range(8)], sign)):
            put(stage, 8 * k + j, rows, turned(value, j * k, BLOCKS, sign))
    for j in range(8):
        outs = small_dft([get(stage, 8 * k + j, rows) for k in range(4)], sign)
        for step, value in enumerate(outs):
            emit(j + 8 * step, value)


def along_lanes(index, source, target, stage, moved):
    inside = lane_ids() % WIDTH
    rows = tile(index)

    def move(freq, value):
        shift, plain, wrapped = shift_of(freq)
        if shift:
            mask = inside >= shift
            value = tuple(
                jnp.where(mask, pltpu.roll(v, shift, 1), pltpu.roll(v, shift + WIDTH, 1))
                for v in value
            )
            real = jnp.where(mask, np.float32(plain.real), np.float32(wrapped.real))
            imag = jnp.where(mask, np.float32(plain.imag), np.float32(wrapped.imag))
            value = times(value, real, imag)
        else:
            value = scaled(value, plain)
        put(moved, freq, rows, value)

    block_dft(lambda block: get(source, block, rows), move, stage, rows, -1)
    block_dft(
        lambda freq: get(moved, freq, rows),
        lambda block, value: put(target, block, rows, value),
        stage,
        rows,
        1,
    )


def along_rows(load, store, stage, held):
    low = lane_ids() < WIDTH
    for index in range(TILES):
        rows = tile(index)

        def hold(freq, value):
            shift, plain, wrapped = shift_of(freq)
            plain = scaled(value, plain)
            wrapped = scaled(value, wrapped) if shift else None
            if shift > HALF:
                put(held, freq, rows, wrapped)
            if shift < HALF:
                put(held, freq, pl.ds(2 * HALF + 8 * index, 8), plain)
            if shift:
                crossed = tuple(
                    pltpu.roll(jnp.where(low, p, w), WIDTH, 1) for p, w in zip(plain, wrapped)
                )
                put(held, freq, pl.ds(HALF + 8 * index, 8), crossed)

        block_dft(functools.partial(load, index), hold, stage, rows, -1)
    for index in range(TILES):
        block_dft(
            lambda freq: get(held, freq, pl.ds(2 * HALF - shift_of(freq)[0] + 8 * index, 8)),
            functools.partial(store, index),
            stage,
            tile(index),
            1,
        )


def natural(index, half):
    return pl.ds(8 * index + HALF * half, 8)


def field_copies(source, target, sems):
    return [
        [
            pltpu.make_async_copy(
                source.at[part, natural(index, half), :],
                target.at[part, natural(index, half), :],
                sems.at[index, part, half],
            )
            for part in range(2)
            for half in range(2)
        ]
        for index in range(TILES)
    ]


def start(copies):
    for tile_copies in copies:
        for copy in tile_copies:
            copy.start()


def wait(tile_copies):
    for copy in tile_copies:
        copy.wait()


def read_field(ref, index, write):
    for pair in range(BLOCKS // 2):
        cols = pl.ds(pair * LANES, LANES)
        parts = [
            halves(ref[part, natural(index, 0), cols], ref[part, natural(index, 1), cols])
            for part in range(2)
        ]
        for side in range(2):
            write(2 * pair + side, (parts[0][side], parts[1][side]))


def enter_kernel(field_ref, other_ref, out_ref, stage, moved):
    grad_out, other_out = out_ref.at[:, 0], out_ref.at[:, 1]
    for index in range(TILES):
        read_field(
            field_ref, index, lambda block, value: put(grad_out, block, tile(index), value)
        )
        along_lanes(index, grad_out, grad_out, stage, moved)
    for index in range(TILES):
        read_field(
            other_ref, index, lambda block, value: put(other_out, block, tile(index), value)
        )


def column_kernel(info_ref, in_ref, wave_ref, out_ref, stage, held):
    use_loss = info_ref[1] == 1
    along_rows(
        lambda index, block: get(in_ref.at[:, 0], block, tile(index)),
        lambda index, block, value: put(wave_ref, block, tile(index), value),
        stage,
        held,
    )

    def passing(index, block):
        real, imag = get(wave_ref, block, tile(index))
        t_real, t_imag = get(in_ref.at[:, 1], block, tile(index))
        return (
            jnp.where(use_loss, t_real, real * t_real + imag * t_imag),
            jnp.where(use_loss, t_imag, imag * t_real - real * t_imag),
        )

    along_rows(
        passing,
        lambda index, block, value: put(out_ref, block, tile(index), value),
        stage,
        held,
    )


def light_tables():
    shifts = np.arange(LED_SIDE) - LED_SIDE // 2
    along_x = np.exp(2j * np.pi * (shifts[:, None] * np.arange(N) % N) / N)
    along_y = np.zeros((WIDTH, LANES), np.complex128)
    along_y[:, :LED_SIDE] = np.exp(2j * np.pi * (np.arange(WIDTH)[:, None] * shifts % N) / N)
    turns = np.exp(2j * np.pi * np.arange(BLOCKS) / BLOCKS)
    return (
        np.concatenate([along_x.real, along_x.imag]).reshape(-1, N // LANES, LANES).astype(np.float32),
        np.stack([along_y.real, along_y.imag]).astype(np.float32),
        np.stack([turns.real, turns.imag]).astype(np.float32),
    )


def light_rows(tick, led_ref, info_ref, turn_ref, lit_y_ref):
    led = led_ref[0, tick]
    column_shift = led // LED_SIDE
    row_shift = led - column_shift * LED_SIDE
    turn = (info_ref[0] * (row_shift - LED_SIDE // 2)) & (BLOCKS - 1)
    turn_real, turn_imag = turn_ref[0, turn], turn_ref[1, turn]
    chosen = lane_ids() == row_shift

    def lit_rows(rows):
        pair = tuple(
            jnp.sum(jnp.where(chosen, lit_y_ref[part, rows, :], 0.0), axis=1, keepdims=True)
            for part in range(2)
        )
        pair = tuple(jnp.broadcast_to(v, (8, LANES)) for v in pair)
        return times(pair, turn_real, turn_imag)

    return column_shift, lit_rows


def write_products(index, wave_ref, lights, lit_x_ref, field_ref, out_ref, *plain):
    column_shift, lit_rows = lights
    lit_y = [lit_rows(natural(index, half)) for half in range(2)]
    for pair in range(BLOCKS // 2):
        cols = pl.ds(pair * LANES, LANES)
        left = get(wave_ref, 2 * pair, tile(index))
        right = get(wave_ref, 2 * pair + 1, tile(index))
        reals, imags = halves(left[0], right[0]), halves(left[1], right[1])
        lit_x = (
            lit_x_ref[column_shift, pair : pair + 1, :],
            lit_x_ref[column_shift + LED_SIDE, pair : pair + 1, :],
        )
        for half in range(2):
            rows = natural(index, half)
            real, imag = reals[half], imags[half]
            if plain:
                t_ref, plain_ref = plain
                t_real, t_imag = t_ref[0, rows, cols], t_ref[1, rows, cols]
                plain_ref[0, rows, cols] = real * t_real + imag * t_imag
                plain_ref[1, rows, cols] = imag * t_real - real * t_imag
            lit = times(lit_y[half], *lit_x)
            f_real, f_imag = times(lit, field_ref[0, rows, cols], field_ref[1, rows, cols])
            out_ref[0, rows, cols] = real * f_real + imag * f_imag
            out_ref[1, rows, cols] = imag * f_real - real * f_imag


def entry_kernel(
    led_ref,
    info_ref,
    turn_ref,
    lit_x_ref,
    lit_y_ref,
    field_ref,
    wave_ref,
    out_hbm,
    out,
    sems,
):
    outs = field_copies(out, out_hbm, sems)
    lights = light_rows(0, led_ref, info_ref, turn_ref, lit_y_ref)
    for index in range(TILES):
        write_products(index, wave_ref, lights, lit_x_ref, field_ref, out)
        start([outs[index]])
    for index in range(TILES):
        wait(outs[index])


def exit_kernel(
    led_ref,
    info_ref,
    turn_ref,
    lit_x_ref,
    lit_y_ref,
    field_ref,
    t_ref,
    in_ref,
    out_hbm,
    plain_hbm,
    packed,
    stage,
    moved,
    out,
    plain,
    out_sems,
    plain_sems,
):
    outs = field_copies(out, out_hbm, out_sems)
    plains = field_copies(plain, plain_hbm, plain_sems)
    lights = light_rows(1, led_ref, info_ref, turn_ref, lit_y_ref)
    for index in range(TILES):
        along_lanes(index, in_ref, packed, stage, moved)
        write_products(index, packed, lights, lit_x_ref, field_ref, out, t_ref, plain)
        start([outs[index], plains[index]])
    for index in range(TILES):
        wait(outs[index] + plains[index])


WHOLE = pl.BlockSpec(memory_space=pltpu.VMEM)
SCALAR = pl.BlockSpec(memory_space=pltpu.SMEM)
OUTSIDE = pl.BlockSpec(memory_space=pltpu.HBM)
CHAIN = (BLOCKS, 2, HALF, LANES)
PACKED = jax.ShapeDtypeStruct(CHAIN, jnp.float32)
BOTH = jax.ShapeDtypeStruct((BLOCKS, 2, 2, HALF, LANES), jnp.float32)
FIELD = jax.ShapeDtypeStruct((2, WIDTH, N), jnp.float32)
FIELD_BUFFER = pltpu.VMEM(FIELD.shape, jnp.float32)
SEMS = pltpu.SemaphoreType.DMA((TILES, 2, 2))
BUFFER = pltpu.VMEM(CHAIN, jnp.float32)
HELD = pltpu.VMEM((BLOCKS, 2, 3 * HALF, LANES), jnp.float32)


def call(kernel, out_shape, operands, name, scratch=(), scalars=0, out_spec=WHOLE):
    outs = jax.tree.leaves(out_shape)
    size = sum(4 * math.prod(x.shape) for x in outs) + sum(4 * x.size for x in operands)
    return pl.pallas_call(
        kernel,
        out_shape=out_shape,
        in_specs=[SCALAR] * scalars + [WHOLE] * (len(operands) - scalars),
        out_specs=jax.tree.map(lambda _: out_spec, out_shape),
        scratch_shapes=list(scratch),
        compiler_params=pltpu.CompilerParams(vmem_limit_bytes=VMEM_LIMIT),
        cost_estimate=pl.CostEstimate(flops=20 * size, bytes_accessed=size, transcendentals=0),
        name=name,
    )(*operands)


def exchange(packed):
    return lax.all_to_all(packed, "rows", split_axis=0, concat_axis=0, tiled=True)


def to_previous(value):
    count = lax.axis_size("depth")
    return lax.ppermute(value, "depth", [(s, (s - 1) % count) for s in range(count)])


def per_device(grad_arriving, loss_grad, t_entry, t_exit, fields_entry, fields_exit, led_index):
    first = (lax.axis_index("depth") == 0).astype(jnp.int32)
    info = jnp.stack([lax.axis_index("rows"), first]).astype(jnp.int32)
    lit_x, lit_y, turns = (jnp.asarray(table) for table in light_tables())
    both = call(
        enter_kernel,
        BOTH,
        [grad_arriving[0], jnp.where(first == 1, loss_grad, t_entry[0])],
        "enter",
        [BUFFER, BUFFER],
    )
    both, info = lax.optimization_barrier((both, info))
    wave, onward = call(
        column_kernel, (PACKED, PACKED), [info, exchange(both)], "columns", [BUFFER, HELD], 1
    )
    onward = to_previous(onward)
    wave = exchange(wave)
    lights = [led_index, info, turns, lit_x, lit_y]
    grad_entry = call(
        entry_kernel,
        FIELD,
        [*lights, fields_entry[0], wave],
        "entry",
        [FIELD_BUFFER, SEMS],
        3,
        OUTSIDE,
    )
    onward, grad_entry = lax.optimization_barrier((onward, grad_entry))
    grad_exit, leaving = call(
        exit_kernel,
        (FIELD, FIELD),
        [*lights, fields_exit[0], t_exit[0], exchange(onward)],
        "exit",
        [BUFFER, BUFFER, BUFFER, FIELD_BUFFER, FIELD_BUFFER, SEMS, SEMS],
        3,
        OUTSIDE,
    )
    return (grad_entry[None], grad_exit[None], leaving[None])


def solution(mesh):
    spread = P("depth", None, "rows", None)
    return jax.shard_map(
        per_device,
        mesh=mesh,
        in_specs=(spread, P(None, "rows", None), spread, spread, spread, spread, P("depth", None)),
        out_specs=(spread, spread, spread),
        check_vma=False,
    )
```

```python
import functools
import math

import jax
import jax.numpy as jnp
import numpy as np
from jax import lax
from jax.experimental import pallas as pl
from jax.experimental.pallas import tpu as pltpu
from jax.sharding import PartitionSpec as P

LED_SIDE = 15
SPREAD = 3
BLOCKS = 32
N = 2048
WIDTH = N // BLOCKS
LANES = 2 * WIDTH
HALF = WIDTH // 2
TILES = HALF // 8
VMEM_LIMIT = 16 * 1024 * 1024

INVERSE = pow(SPREAD, -1, N)
_k = np.arange(N, dtype=np.int64)
GAUSS = np.exp(-2j * np.pi * ((SPREAD * _k * _k) % N) / N).sum() / N


def chirp_gain(distance):
    return complex(GAUSS * np.exp(2j * np.pi * ((INVERSE * distance * distance) % N) / N))


def shift_of(freq):
    pairs = SPREAD * (freq - BLOCKS // 2) % BLOCKS
    return 2 * pairs, chirp_gain(-pairs), chirp_gain(BLOCKS - pairs)


def plus(a, b):
    return (a[0] + b[0], a[1] + b[1])


def minus(a, b):
    return (a[0] - b[0], a[1] - b[1])


def times_i(a):
    return (-a[1], a[0])


def times(a, real, imag):
    return (a[0] * real - a[1] * imag, a[0] * imag + a[1] * real)


def scaled(a, factor):
    return times(a, np.float32(factor.real), np.float32(factor.imag))


def turned(a, step, count, sign):
    step = step * sign % count
    if step == 0:
        return a
    if 2 * step == count:
        return (-a[0], -a[1])
    if 4 * step == count:
        return times_i(a)
    if 4 * step == 3 * count:
        return (a[1], -a[0])
    if 8 * step % count == 0:
        root = np.float32(math.sqrt(0.5))
        eighth = 8 * step // count
        added, taken = (a[0] + a[1]) * root, (a[0] - a[1]) * root
        return {
            1: (taken, added),
            3: (-added, taken),
            5: (-taken, -added),
            7: (added, -taken),
        }[eighth]
    angle = 2.0 * math.pi * step / count
    return scaled(a, complex(math.cos(angle), math.sin(angle)))


def small_dft(values, sign):
    count = len(values)
    if count == 1:
        return values
    if count == 2:
        return [plus(*values), minus(*values)]
    quarter = count // 4
    parts = [small_dft(values[phase::4], sign) for phase in range(4)]
    result = [None] * count
    for j in range(quarter):
        a, b, c, d = (turned(parts[k][j], j * k, count, sign) for k in range(4))
        sum_ac, dif_ac, sum_bd, dif_bd = plus(a, c), minus(a, c), plus(b, d), minus(b, d)
        result[j] = plus(sum_ac, sum_bd)
        result[j + 2 * quarter] = minus(sum_ac, sum_bd)
        up = (dif_ac[0] - dif_bd[1], dif_ac[1] + dif_bd[0])
        down = (dif_ac[0] + dif_bd[1], dif_ac[1] - dif_bd[0])
        result[j + quarter], result[j + 3 * quarter] = (up, down) if sign > 0 else (down, up)
    return result


def lane_ids():
    return lax.broadcasted_iota(jnp.int32, (8, LANES), 1)


def halves(first, second):
    low = lane_ids() < WIDTH
    return (
        jnp.where(low, first, pltpu.roll(second, WIDTH, 1)),
        jnp.where(low, pltpu.roll(first, WIDTH, 1), second),
    )


def tile(index):
    return pl.ds(8 * index, 8)


def get(ref, block, rows):
    return (ref[block, 0, rows, :], ref[block, 1, rows, :])


def put(ref, block, rows, value):
    ref[block, 0, rows, :] = value[0]
    ref[block, 1, rows, :] = value[1]


def block_dft(load, emit, stage, rows, sign):
    for k in range(4):
        for j, value in enumerate(small_dft([load(4 * n + k) for n in range(8)], sign)):
            put(stage, 8 * k + j, rows, turned(value, j * k, BLOCKS, sign))
    for j in range(8):
        outs = small_dft([get(stage, 8 * k + j, rows) for k in range(4)], sign)
        for step, value in enumerate(outs):
            emit(j + 8 * step, value)


def along_lanes(index, source, target, stage, moved):
    inside = lane_ids() % WIDTH
    rows = tile(index)

    def move(freq, value):
        shift, plain, wrapped = shift_of(freq)
        if shift:
            mask = inside >= shift
            value = tuple(
                jnp.where(mask, pltpu.roll(v, shift, 1), pltpu.roll(v, shift + WIDTH, 1))
                for v in value
            )
            real = jnp.where(mask, np.float32(plain.real), np.float32(wrapped.real))
            imag = jnp.where(mask, np.float32(plain.imag), np.float32(wrapped.imag))
            value = times(value, real, imag)
        else:
            value = scaled(value, plain)
        put(moved, freq, rows, value)

    block_dft(lambda block: get(source, block, rows), move, stage, rows, -1)
    block_dft(
        lambda freq: get(moved, freq, rows),
        lambda block, value: put(target, block, rows, value),
        stage,
        rows,
        1,
    )


def along_rows(load, store, stage, held):
    row_ids = lax.broadcasted_iota(jnp.int32, (8, LANES), 0)
    low = lane_ids() < WIDTH
    for index in range(TILES):
        rows = tile(index)

        def hold(freq, value):
            shift = shift_of(freq)[0]
            if shift > HALF:
                put(held, freq, rows, value)
            if shift:
                crossed = tuple(pltpu.roll(v, WIDTH, 1) for v in value)
                put(held, freq, pl.ds(HALF + 8 * index, 8), crossed)
            if shift < HALF:
                put(held, freq, pl.ds(2 * HALF + 8 * index, 8), value)

        block_dft(functools.partial(load, index), hold, stage, rows, -1)

    def shifted(index, freq):
        shift, plain, wrapped = shift_of(freq)
        begin = 2 * HALF - shift + 8 * index
        value = get(held, freq, pl.ds(begin, 8))
        if begin >= 2 * HALF:
            return scaled(value, plain)
        if begin + 8 <= HALF:
            return scaled(value, wrapped)
        mask = row_ids >= jnp.where(low, 2 * HALF - begin, HALF - begin)
        return times(
            value,
            jnp.where(mask, np.float32(plain.real), np.float32(wrapped.real)),
            jnp.where(mask, np.float32(plain.imag), np.float32(wrapped.imag)),
        )

    for index in range(TILES):
        block_dft(
            functools.partial(shifted, index),
            functools.partial(store, index),
            stage,
            tile(index),
            1,
        )


def natural(index, half):
    return pl.ds(8 * index + HALF * half, 8)


def field_copies(source, target, sems):
    return [
        [
            pltpu.make_async_copy(
                source.at[part, natural(index, half), :],
                target.at[part, natural(index, half), :],
                sems.at[index, part, half],
            )
            for part in range(2)
            for half in range(2)
        ]
        for index in range(TILES)
    ]


def start(copies):
    for tile_copies in copies:
        for copy in tile_copies:
            copy.start()


def wait(tile_copies):
    for copy in tile_copies:
        copy.wait()


def read_field(ref, index, write):
    for pair in range(BLOCKS // 2):
        cols = pl.ds(pair * LANES, LANES)
        parts = [
            halves(ref[part, natural(index, 0), cols], ref[part, natural(index, 1), cols])
            for part in range(2)
        ]
        for side in range(2):
            write(2 * pair + side, (parts[0][side], parts[1][side]))


def enter_kernel(field_ref, other_ref, out_ref, stage, moved):
    grad_out, other_out = out_ref.at[:, 0], out_ref.at[:, 1]
    for index in range(TILES):
        read_field(
            field_ref, index, lambda block, value: put(grad_out, block, tile(index), value)
        )
        along_lanes(index, grad_out, grad_out, stage, moved)
    for index in range(TILES):
        read_field(
            other_ref, index, lambda block, value: put(other_out, block, tile(index), value)
        )


def column_kernel(info_ref, in_ref, wave_ref, out_ref, stage, held):
    use_loss = info_ref[1] == 1
    along_rows(
        lambda index, block: get(in_ref.at[:, 0], block, tile(index)),
        lambda index, block, value: put(wave_ref, block, tile(index), value),
        stage,
        held,
    )

    def passing(index, block):
        real, imag = get(wave_ref, block, tile(index))
        t_real, t_imag = get(in_ref.at[:, 1], block, tile(index))
        return (
            jnp.where(use_loss, t_real, real * t_real + imag * t_imag),
            jnp.where(use_loss, t_imag, imag * t_real - real * t_imag),
        )

    along_rows(
        passing,
        lambda index, block, value: put(out_ref, block, tile(index), value),
        stage,
        held,
    )


def light_tables():
    shifts = np.arange(LED_SIDE) - LED_SIDE // 2
    along_x = np.exp(2j * np.pi * (shifts[:, None] * np.arange(N) % N) / N)
    along_y = np.zeros((WIDTH, LANES), np.complex128)
    along_y[:, :LED_SIDE] = np.exp(2j * np.pi * (np.arange(WIDTH)[:, None] * shifts % N) / N)
    turns = np.exp(2j * np.pi * np.arange(BLOCKS) / BLOCKS)
    return (
        np.concatenate([along_x.real, along_x.imag]).reshape(-1, N // LANES, LANES).astype(np.float32),
        np.stack([along_y.real, along_y.imag]).astype(np.float32),
        np.stack([turns.real, turns.imag]).astype(np.float32),
    )


def light_rows(tick, led_ref, info_ref, turn_ref, lit_y_ref):
    led = led_ref[0, tick]
    column_shift = led // LED_SIDE
    row_shift = led - column_shift * LED_SIDE
    turn = (info_ref[0] * (row_shift - LED_SIDE // 2)) & (BLOCKS - 1)
    turn_real, turn_imag = turn_ref[0, turn], turn_ref[1, turn]
    chosen = lane_ids() == row_shift

    def lit_rows(rows):
        pair = tuple(
            jnp.sum(jnp.where(chosen, lit_y_ref[part, rows, :], 0.0), axis=1, keepdims=True)
            for part in range(2)
        )
        pair = tuple(jnp.broadcast_to(v, (8, LANES)) for v in pair)
        return times(pair, turn_real, turn_imag)

    return column_shift, lit_rows


def write_products(index, wave_ref, lights, lit_x_ref, field_ref, out_ref, *plain):
    column_shift, lit_rows = lights
    lit_y = [lit_rows(natural(index, half)) for half in range(2)]
    for pair in range(BLOCKS // 2):
        cols = pl.ds(pair * LANES, LANES)
        left = get(wave_ref, 2 * pair, tile(index))
        right = get(wave_ref, 2 * pair + 1, tile(index))
        reals, imags = halves(left[0], right[0]), halves(left[1], right[1])
        lit_x = (
            lit_x_ref[column_shift, pair : pair + 1, :],
            lit_x_ref[column_shift + LED_SIDE, pair : pair + 1, :],
        )
        for half in range(2):
            rows = natural(index, half)
            real, imag = reals[half], imags[half]
            if plain:
                t_ref, plain_ref = plain
                t_real, t_imag = t_ref[0, rows, cols], t_ref[1, rows, cols]
                plain_ref[0, rows, cols] = real * t_real + imag * t_imag
                plain_ref[1, rows, cols] = imag * t_real - real * t_imag
            lit = times(lit_y[half], *lit_x)
            f_real, f_imag = times(lit, field_ref[0, rows, cols], field_ref[1, rows, cols])
            out_ref[0, rows, cols] = real * f_real + imag * f_imag
            out_ref[1, rows, cols] = imag * f_real - real * f_imag


def last_kernel(
    led_ref,
    info_ref,
    turn_ref,
    lit_x_ref,
    lit_y_ref,
    entry_ref,
    exit_ref,
    t_ref,
    wave_ref,
    onward_ref,
    entry_hbm,
    exit_hbm,
    plain_hbm,
    packed,
    stage,
    moved,
    entry_out,
    exit_out,
    plain_out,
    *sems,
):
    results = ((entry_out, entry_hbm), (exit_out, exit_hbm), (plain_out, plain_hbm))
    outs = [field_copies(*pair, sem) for pair, sem in zip(results, sems)]
    lights = [light_rows(tick, led_ref, info_ref, turn_ref, lit_y_ref) for tick in range(2)]
    for index in range(TILES):
        write_products(index, wave_ref, lights[0], lit_x_ref, entry_ref, entry_out)
        start([outs[0][index]])
        along_lanes(index, onward_ref, packed, stage, moved)
        write_products(index, packed, lights[1], lit_x_ref, exit_ref, exit_out, t_ref, plain_out)
        start([outs[1][index], outs[2][index]])
    for index in range(TILES):
        wait(outs[0][index] + outs[1][index] + outs[2][index])


WHOLE = pl.BlockSpec(memory_space=pltpu.VMEM)
SCALAR = pl.BlockSpec(memory_space=pltpu.SMEM)
OUTSIDE = pl.BlockSpec(memory_space=pltpu.HBM)
CHAIN = (BLOCKS, 2, HALF, LANES)
PACKED = jax.ShapeDtypeStruct(CHAIN, jnp.float32)
BOTH = jax.ShapeDtypeStruct((BLOCKS, 2, 2, HALF, LANES), jnp.float32)
FIELD = jax.ShapeDtypeStruct((2, WIDTH, N), jnp.float32)
FIELD_BUFFER = pltpu.VMEM(FIELD.shape, jnp.float32)
SEMS = pltpu.SemaphoreType.DMA((TILES, 2, 2))
BUFFER = pltpu.VMEM(CHAIN, jnp.float32)
HELD = pltpu.VMEM((BLOCKS, 2, 3 * HALF, LANES), jnp.float32)


def call(kernel, out_shape, operands, name, scratch=(), scalars=0, out_spec=WHOLE):
    outs = jax.tree.leaves(out_shape)
    size = sum(4 * math.prod(x.shape) for x in outs) + sum(4 * x.size for x in operands)
    return pl.pallas_call(
        kernel,
        out_shape=out_shape,
        in_specs=[SCALAR] * scalars + [WHOLE] * (len(operands) - scalars),
        out_specs=jax.tree.map(lambda _: out_spec, out_shape),
        scratch_shapes=list(scratch),
        compiler_params=pltpu.CompilerParams(vmem_limit_bytes=VMEM_LIMIT),
        cost_estimate=pl.CostEstimate(flops=20 * size, bytes_accessed=size, transcendentals=0),
        name=name,
    )(*operands)


def exchange(packed):
    return lax.all_to_all(packed, "rows", split_axis=0, concat_axis=0, tiled=True)


def to_previous(value):
    count = lax.axis_size("depth")
    return lax.ppermute(value, "depth", [(s, (s - 1) % count) for s in range(count)])


def per_device(grad_arriving, loss_grad, t_entry, t_exit, fields_entry, fields_exit, led_index):
    first = (lax.axis_index("depth") == 0).astype(jnp.int32)
    info = jnp.stack([lax.axis_index("rows"), first]).astype(jnp.int32)
    lit_x, lit_y, turns = (jnp.asarray(table) for table in light_tables())
    both = call(
        enter_kernel,
        BOTH,
        [grad_arriving[0], jnp.where(first == 1, loss_grad, t_entry[0])],
        "enter",
        [BUFFER, BUFFER],
    )
    both, info = lax.optimization_barrier((both, info))
    wave, onward = call(
        column_kernel, (PACKED, PACKED), [info, exchange(both)], "columns", [BUFFER, HELD], 1
    )
    onward = exchange(onward)
    wave, onward = lax.optimization_barrier((wave, onward))
    onward = to_previous(onward)
    wave = exchange(wave)
    grad_entry, grad_exit, leaving = call(
        last_kernel,
        (FIELD, FIELD, FIELD),
        [
            led_index,
            info,
            turns,
            lit_x,
            lit_y,
            fields_entry[0],
            fields_exit[0],
            t_exit[0],
            wave,
            onward,
        ],
        "last",
        [BUFFER] * 3 + [FIELD_BUFFER] * 3 + [SEMS] * 3,
        3,
        OUTSIDE,
    )
    return (grad_entry[None], grad_exit[None], leaving[None])


def solution(mesh):
    spread = P("depth", None, "rows", None)
    return jax.shard_map(
        per_device,
        mesh=mesh,
        in_specs=(spread, P(None, "rows", None), spread, spread, spread, spread, P("depth", None)),
        out_specs=(spread, spread, spread),
        check_vma=False,
    )
```

```python
import functools
import math

import jax
import jax.numpy as jnp
import numpy as np
from jax import lax
from jax.experimental import pallas as pl
from jax.experimental.pallas import tpu as pltpu
from jax.sharding import PartitionSpec as P

LED_SIDE = 15
SPREAD = 3
BLOCKS = 32
N = 2048
WIDTH = N // BLOCKS
LANES = 2 * WIDTH
HALF = WIDTH // 2
TILES = HALF // 8
VMEM_LIMIT = 16 * 1024 * 1024

INVERSE = pow(SPREAD, -1, N)
_k = np.arange(N, dtype=np.int64)
GAUSS = np.exp(-2j * np.pi * ((SPREAD * _k * _k) % N) / N).sum() / N


def chirp_gain(distance):
    return complex(GAUSS * np.exp(2j * np.pi * ((INVERSE * distance * distance) % N) / N))


def shift_of(freq):
    pairs = SPREAD * (freq - BLOCKS // 2) % BLOCKS
    return 2 * pairs, chirp_gain(-pairs), chirp_gain(BLOCKS - pairs)


def plus(a, b):
    return (a[0] + b[0], a[1] + b[1])


def minus(a, b):
    return (a[0] - b[0], a[1] - b[1])


def times_i(a):
    return (-a[1], a[0])


def times(a, real, imag):
    return (a[0] * real - a[1] * imag, a[0] * imag + a[1] * real)


def scaled(a, factor):
    return times(a, np.float32(factor.real), np.float32(factor.imag))


def turned(a, step, count, sign):
    step = step * sign % count
    if step == 0:
        return a
    if 2 * step == count:
        return (-a[0], -a[1])
    if 4 * step == count:
        return times_i(a)
    if 4 * step == 3 * count:
        return (a[1], -a[0])
    if 8 * step % count == 0:
        root = np.float32(math.sqrt(0.5))
        eighth = 8 * step // count
        added, taken = (a[0] + a[1]) * root, (a[0] - a[1]) * root
        return {
            1: (taken, added),
            3: (-added, taken),
            5: (-taken, -added),
            7: (added, -taken),
        }[eighth]
    angle = 2.0 * math.pi * step / count
    return scaled(a, complex(math.cos(angle), math.sin(angle)))


def small_dft(values, sign):
    count = len(values)
    if count == 1:
        return values
    if count == 2:
        return [plus(*values), minus(*values)]
    quarter = count // 4
    parts = [small_dft(values[phase::4], sign) for phase in range(4)]
    result = [None] * count
    for j in range(quarter):
        a, b, c, d = (turned(parts[k][j], j * k, count, sign) for k in range(4))
        sum_ac, dif_ac, sum_bd, dif_bd = plus(a, c), minus(a, c), plus(b, d), minus(b, d)
        result[j] = plus(sum_ac, sum_bd)
        result[j + 2 * quarter] = minus(sum_ac, sum_bd)
        up = (dif_ac[0] - dif_bd[1], dif_ac[1] + dif_bd[0])
        down = (dif_ac[0] + dif_bd[1], dif_ac[1] - dif_bd[0])
        result[j + quarter], result[j + 3 * quarter] = (up, down) if sign > 0 else (down, up)
    return result


def lane_ids():
    return lax.broadcasted_iota(jnp.int32, (8, LANES), 1)


def halves(first, second):
    low = lane_ids() < WIDTH
    return (
        jnp.where(low, first, pltpu.roll(second, WIDTH, 1)),
        jnp.where(low, pltpu.roll(first, WIDTH, 1), second),
    )


def tile(index):
    return pl.ds(8 * index, 8)


def get(ref, block, rows):
    return (ref[block, 0, rows, :], ref[block, 1, rows, :])


def put(ref, block, rows, value):
    ref[block, 0, rows, :] = value[0]
    ref[block, 1, rows, :] = value[1]


def block_dft(load, emit, stage, rows, sign):
    for k in range(4):
        for j, value in enumerate(small_dft([load(4 * n + k) for n in range(8)], sign)):
            put(stage, 8 * k + j, rows, turned(value, j * k, BLOCKS, sign))
    for j in range(8):
        outs = small_dft([get(stage, 8 * k + j, rows) for k in range(4)], sign)
        for step, value in enumerate(outs):
            emit(j + 8 * step, value)


def along_lanes(index, source, target, stage, moved, place=None):
    inside = lane_ids() % WIDTH
    rows = tile(index)
    source_rows = rows if place is None else tile(place)

    def move(freq, value):
        shift, plain, wrapped = shift_of(freq)
        if shift:
            mask = inside >= shift
            value = tuple(
                jnp.where(mask, pltpu.roll(v, shift, 1), pltpu.roll(v, shift + WIDTH, 1))
                for v in value
            )
            real = jnp.where(mask, np.float32(plain.real), np.float32(wrapped.real))
            imag = jnp.where(mask, np.float32(plain.imag), np.float32(wrapped.imag))
            value = times(value, real, imag)
        else:
            value = scaled(value, plain)
        put(moved, freq, rows, value)

    block_dft(lambda block: get(source, block, source_rows), move, stage, rows, -1)
    block_dft(
        lambda freq: get(moved, freq, rows),
        lambda block, value: put(target, block, rows, value),
        stage,
        rows,
        1,
    )


def along_rows(load, store, stage, held):
    row_ids = lax.broadcasted_iota(jnp.int32, (8, LANES), 0)
    low = lane_ids() < WIDTH
    for index in range(TILES):
        rows = tile(index)

        def hold(freq, value):
            shift = shift_of(freq)[0]
            if shift > HALF:
                put(held, freq, rows, value)
            if shift:
                crossed = tuple(pltpu.roll(v, WIDTH, 1) for v in value)
                put(held, freq, pl.ds(HALF + 8 * index, 8), crossed)
            if shift < HALF:
                put(held, freq, pl.ds(2 * HALF + 8 * index, 8), value)

        block_dft(functools.partial(load, index), hold, stage, rows, -1)

    def shifted(index, freq):
        shift, plain, wrapped = shift_of(freq)
        begin = 2 * HALF - shift + 8 * index
        value = get(held, freq, pl.ds(begin, 8))
        if begin >= 2 * HALF:
            return scaled(value, plain)
        if begin + 8 <= HALF:
            return scaled(value, wrapped)
        mask = row_ids >= jnp.where(low, 2 * HALF - begin, HALF - begin)
        return times(
            value,
            jnp.where(mask, np.float32(plain.real), np.float32(wrapped.real)),
            jnp.where(mask, np.float32(plain.imag), np.float32(wrapped.imag)),
        )

    for index in range(TILES):
        block_dft(
            functools.partial(shifted, index),
            functools.partial(store, index),
            stage,
            tile(index),
            1,
        )


def natural(index, half):
    return pl.ds(8 * index + HALF * half, 8)


def field_copies(source, target, sems):
    return [
        [
            pltpu.make_async_copy(
                source.at[part, natural(index, half), :],
                target.at[part, natural(index, half), :],
                sems.at[index, part, half],
            )
            for part in range(2)
            for half in range(2)
        ]
        for index in range(TILES)
    ]


def start(copies):
    for tile_copies in copies:
        for copy in tile_copies:
            copy.start()


def wait(tile_copies):
    for copy in tile_copies:
        copy.wait()


def read_field(ref, index, write):
    for pair in range(BLOCKS // 2):
        cols = pl.ds(pair * LANES, LANES)
        parts = [
            halves(ref[part, natural(index, 0), cols], ref[part, natural(index, 1), cols])
            for part in range(2)
        ]
        for side in range(2):
            write(2 * pair + side, (parts[0][side], parts[1][side]))


def enter_kernel(field_ref, other_ref, out_ref, stage, moved):
    grad_out, other_out = out_ref.at[:, 0], out_ref.at[:, 1]
    for index in range(TILES):
        read_field(
            field_ref, index, lambda block, value: put(grad_out, block, tile(index), value)
        )
        along_lanes(index, grad_out, grad_out, stage, moved)
    for index in range(TILES):
        read_field(
            other_ref, index, lambda block, value: put(other_out, block, tile(index), value)
        )


def column_kernel(info_ref, in_ref, near_ref, far_ref, stage, held):
    use_loss = info_ref[1] == 1

    def put_wave(index, block, value):
        put(near_ref, block, tile(index), value)

    def put_onward(index, block, value):
        if index < FAR:
            put(far_ref, block, tile(index), value)
        else:
            put(near_ref, block, tile(TILES + index - FAR), value)

    def passing(index, block):
        real, imag = get(near_ref, block, tile(index))
        t_real, t_imag = get(in_ref.at[:, 1], block, tile(index))
        return (
            jnp.where(use_loss, t_real, real * t_real + imag * t_imag),
            jnp.where(use_loss, t_imag, imag * t_real - real * t_imag),
        )

    along_rows(
        lambda index, block: get(in_ref.at[:, 0], block, tile(index)), put_wave, stage, held
    )
    along_rows(passing, put_onward, stage, held)


def light_tables():
    shifts = np.arange(LED_SIDE) - LED_SIDE // 2
    along_x = np.exp(2j * np.pi * (shifts[:, None] * np.arange(N) % N) / N)
    along_y = np.zeros((WIDTH, LANES), np.complex128)
    along_y[:, :LED_SIDE] = np.exp(2j * np.pi * (np.arange(WIDTH)[:, None] * shifts % N) / N)
    turns = np.exp(2j * np.pi * np.arange(BLOCKS) / BLOCKS)
    return (
        np.concatenate([along_x.real, along_x.imag]).reshape(-1, N // LANES, LANES).astype(np.float32),
        np.stack([along_y.real, along_y.imag]).astype(np.float32),
        np.stack([turns.real, turns.imag]).astype(np.float32),
    )


def light_rows(tick, led_ref, info_ref, turn_ref, lit_y_ref):
    led = led_ref[0, tick]
    column_shift = led // LED_SIDE
    row_shift = led - column_shift * LED_SIDE
    turn = (info_ref[0] * (row_shift - LED_SIDE // 2)) & (BLOCKS - 1)
    turn_real, turn_imag = turn_ref[0, turn], turn_ref[1, turn]
    chosen = lane_ids() == row_shift

    def lit_rows(rows):
        pair = tuple(
            jnp.sum(jnp.where(chosen, lit_y_ref[part, rows, :], 0.0), axis=1, keepdims=True)
            for part in range(2)
        )
        pair = tuple(jnp.broadcast_to(v, (8, LANES)) for v in pair)
        return times(pair, turn_real, turn_imag)

    return column_shift, lit_rows


def write_products(index, wave_ref, lights, lit_x_ref, field_ref, out_ref, *plain):
    column_shift, lit_rows = lights
    lit_y = [lit_rows(natural(index, half)) for half in range(2)]
    for pair in range(BLOCKS // 2):
        cols = pl.ds(pair * LANES, LANES)
        left = get(wave_ref, 2 * pair, tile(index))
        right = get(wave_ref, 2 * pair + 1, tile(index))
        reals, imags = halves(left[0], right[0]), halves(left[1], right[1])
        lit_x = (
            lit_x_ref[column_shift, pair : pair + 1, :],
            lit_x_ref[column_shift + LED_SIDE, pair : pair + 1, :],
        )
        for half in range(2):
            rows = natural(index, half)
            real, imag = reals[half], imags[half]
            if plain:
                t_ref, plain_ref = plain
                t_real, t_imag = t_ref[0, rows, cols], t_ref[1, rows, cols]
                plain_ref[0, rows, cols] = real * t_real + imag * t_imag
                plain_ref[1, rows, cols] = imag * t_real - real * t_imag
            lit = times(lit_y[half], *lit_x)
            f_real, f_imag = times(lit, field_ref[0, rows, cols], field_ref[1, rows, cols])
            out_ref[0, rows, cols] = real * f_real + imag * f_imag
            out_ref[1, rows, cols] = imag * f_real - real * f_imag


def last_kernel(
    led_ref,
    info_ref,
    turn_ref,
    lit_x_ref,
    lit_y_ref,
    entry_ref,
    exit_ref,
    t_ref,
    wave_ref,
    far_ref,
    near_ref,
    entry_hbm,
    exit_hbm,
    plain_hbm,
    packed,
    stage,
    moved,
    entry_out,
    exit_out,
    plain_out,
    *sems,
):
    results = ((entry_out, entry_hbm), (exit_out, exit_hbm), (plain_out, plain_hbm))
    outs = [field_copies(*pair, sem) for pair, sem in zip(results, sems)]
    lights = [light_rows(tick, led_ref, info_ref, turn_ref, lit_y_ref) for tick in range(2)]
    for index in range(TILES):
        write_products(index, wave_ref, lights[0], lit_x_ref, entry_ref, entry_out)
        start([outs[0][index]])
        source, place = (far_ref, index) if index < FAR else (near_ref, index - FAR)
        along_lanes(index, source, packed, stage, moved, place)
        write_products(index, packed, lights[1], lit_x_ref, exit_ref, exit_out, t_ref, plain_out)
        start([outs[1][index], outs[2][index]])
    for index in range(TILES):
        wait(outs[0][index] + outs[1][index] + outs[2][index])


WHOLE = pl.BlockSpec(memory_space=pltpu.VMEM)
SCALAR = pl.BlockSpec(memory_space=pltpu.SMEM)
OUTSIDE = pl.BlockSpec(memory_space=pltpu.HBM)
FAR = TILES // 2
CHAIN = (BLOCKS, 2, HALF, LANES)
NEAR_SHAPE = jax.ShapeDtypeStruct((BLOCKS, 2, 2 * HALF - 8 * FAR, LANES), jnp.float32)
FAR_SHAPE = jax.ShapeDtypeStruct((BLOCKS, 2, 8 * FAR, LANES), jnp.float32)
BOTH = jax.ShapeDtypeStruct((BLOCKS, 2, 2, HALF, LANES), jnp.float32)
FIELD = jax.ShapeDtypeStruct((2, WIDTH, N), jnp.float32)
FIELD_BUFFER = pltpu.VMEM(FIELD.shape, jnp.float32)
SEMS = pltpu.SemaphoreType.DMA((TILES, 2, 2))
BUFFER = pltpu.VMEM(CHAIN, jnp.float32)
HELD = pltpu.VMEM((BLOCKS, 2, 3 * HALF, LANES), jnp.float32)


def call(kernel, out_shape, operands, name, scratch=(), scalars=0, out_spec=WHOLE):
    outs = jax.tree.leaves(out_shape)
    size = sum(4 * math.prod(x.shape) for x in outs) + sum(4 * x.size for x in operands)
    return pl.pallas_call(
        kernel,
        out_shape=out_shape,
        in_specs=[SCALAR] * scalars + [WHOLE] * (len(operands) - scalars),
        out_specs=jax.tree.map(lambda _: out_spec, out_shape),
        scratch_shapes=list(scratch),
        compiler_params=pltpu.CompilerParams(vmem_limit_bytes=VMEM_LIMIT),
        cost_estimate=pl.CostEstimate(flops=20 * size, bytes_accessed=size, transcendentals=0),
        name=name,
    )(*operands)


def exchange(packed):
    return lax.all_to_all(packed, "rows", split_axis=0, concat_axis=0, tiled=True)


def to_previous(value):
    count = lax.axis_size("depth")
    return lax.ppermute(value, "depth", [(s, (s - 1) % count) for s in range(count)])


def per_device(grad_arriving, loss_grad, t_entry, t_exit, fields_entry, fields_exit, led_index):
    first = (lax.axis_index("depth") == 0).astype(jnp.int32)
    info = jnp.stack([lax.axis_index("rows"), first]).astype(jnp.int32)
    lit_x, lit_y, turns = (jnp.asarray(table) for table in light_tables())
    both = call(
        enter_kernel,
        BOTH,
        [grad_arriving[0], jnp.where(first == 1, loss_grad, t_entry[0])],
        "enter",
        [BUFFER, BUFFER],
    )
    both, info = lax.optimization_barrier((both, info))
    near, far = call(
        column_kernel,
        (NEAR_SHAPE, FAR_SHAPE),
        [info, exchange(both)],
        "columns",
        [BUFFER, HELD],
        1,
    )
    far = to_previous(far)
    near = exchange(near)
    near, far = lax.optimization_barrier((near, far))
    onward = to_previous(near[:, :, HALF:, :])
    grad_entry, grad_exit, leaving = call(
        last_kernel,
        (FIELD, FIELD, FIELD),
        [
            led_index,
            info,
            turns,
            lit_x,
            lit_y,
            fields_entry[0],
            fields_exit[0],
            t_exit[0],
            near,
            exchange(far),
            onward,
        ],
        "last",
        [BUFFER] * 3 + [FIELD_BUFFER] * 3 + [SEMS] * 3,
        3,
        OUTSIDE,
    )
    return (grad_entry[None], grad_exit[None], leaving[None])


def solution(mesh):
    spread = P("depth", None, "rows", None)
    return jax.shard_map(
        per_device,
        mesh=mesh,
        in_specs=(spread, P(None, "rows", None), spread, spread, spread, spread, P("depth", None)),
        out_specs=(spread, spread, spread),
        check_vma=False,
    )
```

```python
import functools
import math

import jax
import jax.numpy as jnp
import numpy as np
from jax import lax
from jax.experimental import pallas as pl
from jax.experimental.pallas import tpu as pltpu
from jax.sharding import PartitionSpec as P

LED_SIDE = 15
SPREAD = 3
BLOCKS = 32
N = 2048
WIDTH = N // BLOCKS
LANES = 2 * WIDTH
HALF = WIDTH // 2
TILES = HALF // 8
VMEM_LIMIT = 16 * 1024 * 1024

INVERSE = pow(SPREAD, -1, N)
_k = np.arange(N, dtype=np.int64)
GAUSS = np.exp(-2j * np.pi * ((SPREAD * _k * _k) % N) / N).sum() / N


def chirp_gain(distance):
    return complex(GAUSS * np.exp(2j * np.pi * ((INVERSE * distance * distance) % N) / N))


def shift_of(freq):
    pairs = SPREAD * (freq - BLOCKS // 2) % BLOCKS
    return 2 * pairs, chirp_gain(-pairs), chirp_gain(BLOCKS - pairs)


def plus(a, b):
    return (a[0] + b[0], a[1] + b[1])


def minus(a, b):
    return (a[0] - b[0], a[1] - b[1])


def times_i(a):
    return (-a[1], a[0])


def times(a, real, imag):
    return (a[0] * real - a[1] * imag, a[0] * imag + a[1] * real)


def scaled(a, factor):
    return times(a, np.float32(factor.real), np.float32(factor.imag))


def turned(a, step, count, sign):
    step = step * sign % count
    if step == 0:
        return a
    if 2 * step == count:
        return (-a[0], -a[1])
    if 4 * step == count:
        return times_i(a)
    if 4 * step == 3 * count:
        return (a[1], -a[0])
    if 8 * step % count == 0:
        root = np.float32(math.sqrt(0.5))
        eighth = 8 * step // count
        added, taken = (a[0] + a[1]) * root, (a[0] - a[1]) * root
        return {
            1: (taken, added),
            3: (-added, taken),
            5: (-taken, -added),
            7: (added, -taken),
        }[eighth]
    angle = 2.0 * math.pi * step / count
    return scaled(a, complex(math.cos(angle), math.sin(angle)))


def small_dft(values, sign):
    count = len(values)
    if count == 1:
        return values
    if count == 2:
        return [plus(*values), minus(*values)]
    quarter = count // 4
    parts = [small_dft(values[phase::4], sign) for phase in range(4)]
    result = [None] * count
    for j in range(quarter):
        a, b, c, d = (turned(parts[k][j], j * k, count, sign) for k in range(4))
        sum_ac, dif_ac, sum_bd, dif_bd = plus(a, c), minus(a, c), plus(b, d), minus(b, d)
        result[j] = plus(sum_ac, sum_bd)
        result[j + 2 * quarter] = minus(sum_ac, sum_bd)
        up = (dif_ac[0] - dif_bd[1], dif_ac[1] + dif_bd[0])
        down = (dif_ac[0] + dif_bd[1], dif_ac[1] - dif_bd[0])
        result[j + quarter], result[j + 3 * quarter] = (up, down) if sign > 0 else (down, up)
    return result


def lane_ids():
    return lax.broadcasted_iota(jnp.int32, (8, LANES), 1)


def halves(first, second):
    low = lane_ids() < WIDTH
    return (
        jnp.where(low, first, pltpu.roll(second, WIDTH, 1)),
        jnp.where(low, pltpu.roll(first, WIDTH, 1), second),
    )


def tile(index):
    return pl.ds(8 * index, 8)


def get(ref, block, rows):
    return (ref[block, 0, rows, :], ref[block, 1, rows, :])


def put(ref, block, rows, value):
    ref[block, 0, rows, :] = value[0]
    ref[block, 1, rows, :] = value[1]


def block_dft(load, emit, stage, rows, sign):
    for k in range(4):
        for j, value in enumerate(small_dft([load(4 * n + k) for n in range(8)], sign)):
            put(stage, 8 * k + j, rows, turned(value, j * k, BLOCKS, sign))
    for j in range(8):
        outs = small_dft([get(stage, 8 * k + j, rows) for k in range(4)], sign)
        for step, value in enumerate(outs):
            emit(j + 8 * step, value)


def along_lanes(index, source, target, stage, moved):
    inside = lane_ids() % WIDTH
    rows = tile(index)

    def move(freq, value):
        shift, plain, wrapped = shift_of(freq)
        if shift:
            mask = inside >= shift
            value = tuple(
                jnp.where(mask, pltpu.roll(v, shift, 1), pltpu.roll(v, shift + WIDTH, 1))
                for v in value
            )
            real = jnp.where(mask, np.float32(plain.real), np.float32(wrapped.real))
            imag = jnp.where(mask, np.float32(plain.imag), np.float32(wrapped.imag))
            value = times(value, real, imag)
        else:
            value = scaled(value, plain)
        put(moved, freq, rows, value)

    block_dft(lambda block: get(source, block, rows), move, stage, rows, -1)
    block_dft(
        lambda freq: get(moved, freq, rows),
        lambda block, value: put(target, block, rows, value),
        stage,
        rows,
        1,
    )


def along_rows(load, store, stage, held):
    row_ids = lax.broadcasted_iota(jnp.int32, (8, LANES), 0)
    low = lane_ids() < WIDTH
    for index in range(TILES):
        rows = tile(index)

        def hold(freq, value):
            shift = shift_of(freq)[0]
            if shift > HALF:
                put(held, freq, rows, value)
            if shift:
                crossed = tuple(pltpu.roll(v, WIDTH, 1) for v in value)
                put(held, freq, pl.ds(HALF + 8 * index, 8), crossed)
            if shift < HALF:
                put(held, freq, pl.ds(2 * HALF + 8 * index, 8), value)

        block_dft(functools.partial(load, index), hold, stage, rows, -1)

    def shifted(index, freq):
        shift, plain, wrapped = shift_of(freq)
        begin = 2 * HALF - shift + 8 * index
        value = get(held, freq, pl.ds(begin, 8))
        if begin >= 2 * HALF:
            return scaled(value, plain)
        if begin + 8 <= HALF:
            return scaled(value, wrapped)
        mask = row_ids >= jnp.where(low, 2 * HALF - begin, HALF - begin)
        return times(
            value,
            jnp.where(mask, np.float32(plain.real), np.float32(wrapped.real)),
            jnp.where(mask, np.float32(plain.imag), np.float32(wrapped.imag)),
        )

    for index in range(TILES):
        block_dft(
            functools.partial(shifted, index),
            functools.partial(store, index),
            stage,
            tile(index),
            1,
        )


def natural(index, half):
    return pl.ds(8 * index + HALF * half, 8)


def field_copies(source, target, sems):
    return [
        [
            pltpu.make_async_copy(
                source.at[part, natural(index, half), :],
                target.at[part, natural(index, half), :],
                sems.at[index, part, half],
            )
            for part in range(2)
            for half in range(2)
        ]
        for index in range(TILES)
    ]


def start(copies):
    for tile_copies in copies:
        for copy in tile_copies:
            copy.start()


def wait(tile_copies):
    for copy in tile_copies:
        copy.wait()


def read_field(ref, index, write):
    for pair in range(BLOCKS // 2):
        cols = pl.ds(pair * LANES, LANES)
        parts = [
            halves(ref[part, natural(index, 0), cols], ref[part, natural(index, 1), cols])
            for part in range(2)
        ]
        for side in range(2):
            write(2 * pair + side, (parts[0][side], parts[1][side]))


def enter_kernel(field_ref, other_ref, out_ref, stage, moved):
    grad_out, other_out = out_ref.at[:, 0], out_ref.at[:, 1]
    for index in range(TILES):
        read_field(
            field_ref, index, lambda block, value: put(grad_out, block, tile(index), value)
        )
        along_lanes(index, grad_out, grad_out, stage, moved)
    for index in range(TILES):
        read_field(
            other_ref, index, lambda block, value: put(other_out, block, tile(index), value)
        )


def column_kernel(
    led_ref,
    info_ref,
    turn_ref,
    all_x_ref,
    all_y_ref,
    in_ref,
    wave_ref,
    out_ref,
    lit_x_ref,
    lit_y_ref,
    stage,
    held,
):
    use_loss = info_ref[1] == 1
    along_rows(
        lambda index, block: get(in_ref.at[:, 0], block, tile(index)),
        lambda index, block, value: put(wave_ref, block, tile(index), value),
        stage,
        held,
    )

    def passing(index, block):
        real, imag = get(wave_ref, block, tile(index))
        t_real, t_imag = get(in_ref.at[:, 1], block, tile(index))
        return (
            jnp.where(use_loss, t_real, real * t_real + imag * t_imag),
            jnp.where(use_loss, t_imag, imag * t_real - real * t_imag),
        )

    along_rows(
        passing,
        lambda index, block, value: put(out_ref, block, tile(index), value),
        stage,
        held,
    )
    for tick in range(2):
        write_light(tick, led_ref, info_ref, turn_ref, all_x_ref, all_y_ref, lit_x_ref, lit_y_ref)


def light_tables():
    shifts = np.arange(LED_SIDE) - LED_SIDE // 2
    along_x = np.exp(2j * np.pi * (shifts[:, None] * np.arange(N) % N) / N)
    along_y = np.zeros((WIDTH, LANES), np.complex128)
    along_y[:, :LED_SIDE] = np.exp(2j * np.pi * (np.arange(WIDTH)[:, None] * shifts % N) / N)
    turns = np.exp(2j * np.pi * np.arange(BLOCKS) / BLOCKS)
    return (
        np.concatenate([along_x.real, along_x.imag]).reshape(-1, N // LANES, LANES).astype(np.float32),
        np.stack([along_y.real, along_y.imag]).astype(np.float32),
        np.stack([np.tile(part[:, None], LANES) for part in (turns.real, turns.imag)]).astype(
            np.float32
        ),
    )


def write_light(
    tick, led_ref, info_ref, turn_ref, all_x_ref, all_y_ref, lit_x_ref, lit_y_ref
):
    led = led_ref[0, tick]
    column_shift = led // LED_SIDE
    row_shift = led - column_shift * LED_SIDE
    turn = (info_ref[0] * (row_shift - LED_SIDE // 2)) & (BLOCKS - 1)
    turns = [turn_ref[part, pl.ds(turn, 1), :] for part in range(2)]
    chosen = lane_ids() == row_shift
    for part in range(2):
        lit_x_ref[tick, part] = all_x_ref[column_shift + part * LED_SIDE]
    for index in range(WIDTH // 8):
        rows = tile(index)
        pair = tuple(
            jnp.sum(jnp.where(chosen, all_y_ref[part, rows, :], 0.0), axis=1, keepdims=True)
            for part in range(2)
        )
        pair = times(tuple(jnp.broadcast_to(v, (8, LANES)) for v in pair), *turns)
        for part in range(2):
            lit_y_ref[tick, part, rows, :] = pair[part]


def write_products(tick, index, wave_ref, lit_x_ref, lit_y_ref, field_ref, out_ref, *plain):
    lit_y = [
        [lit_y_ref[tick, part, natural(index, half), :] for part in range(2)]
        for half in range(2)
    ]
    for pair in range(BLOCKS // 2):
        cols = pl.ds(pair * LANES, LANES)
        left = get(wave_ref, 2 * pair, tile(index))
        right = get(wave_ref, 2 * pair + 1, tile(index))
        reals, imags = halves(left[0], right[0]), halves(left[1], right[1])
        lit_x = [lit_x_ref[tick, part, pair : pair + 1, :] for part in range(2)]
        for half in range(2):
            rows = natural(index, half)
            real, imag = reals[half], imags[half]
            if plain:
                t_ref, plain_ref = plain
                t_real, t_imag = t_ref[0, rows, cols], t_ref[1, rows, cols]
                plain_ref[0, rows, cols] = real * t_real + imag * t_imag
                plain_ref[1, rows, cols] = imag * t_real - real * t_imag
            lit = times(lit_y[half], *lit_x)
            f_real, f_imag = times(lit, field_ref[0, rows, cols], field_ref[1, rows, cols])
            out_ref[0, rows, cols] = real * f_real + imag * f_imag
            out_ref[1, rows, cols] = imag * f_real - real * f_imag


def entry_kernel(lit_x_ref, lit_y_ref, field_ref, wave_ref, out_hbm, out, sems):
    outs = field_copies(out, out_hbm, sems)
    for index in range(TILES):
        write_products(0, index, wave_ref, lit_x_ref, lit_y_ref, field_ref, out)
        start([outs[index]])
    for index in range(TILES):
        wait(outs[index])


def exit_kernel(
    lit_x_ref,
    lit_y_ref,
    field_ref,
    t_ref,
    in_ref,
    out_hbm,
    plain_hbm,
    packed,
    stage,
    moved,
    out,
    plain,
    out_sems,
    plain_sems,
):
    outs = field_copies(out, out_hbm, out_sems)
    plains = field_copies(plain, plain_hbm, plain_sems)
    for index in range(TILES):
        along_lanes(index, in_ref, packed, stage, moved)
        write_products(1, index, packed, lit_x_ref, lit_y_ref, field_ref, out, t_ref, plain)
        start([outs[index], plains[index]])
    for index in range(TILES):
        wait(outs[index] + plains[index])


WHOLE = pl.BlockSpec(memory_space=pltpu.VMEM)
SCALAR = pl.BlockSpec(memory_space=pltpu.SMEM)
OUTSIDE = pl.BlockSpec(memory_space=pltpu.HBM)
CHAIN = (BLOCKS, 2, HALF, LANES)
PACKED = jax.ShapeDtypeStruct(CHAIN, jnp.float32)
LIT_X = jax.ShapeDtypeStruct((2, 2, N // LANES, LANES), jnp.float32)
LIT_Y = jax.ShapeDtypeStruct((2, 2, WIDTH, LANES), jnp.float32)
BOTH = jax.ShapeDtypeStruct((BLOCKS, 2, 2, HALF, LANES), jnp.float32)
FIELD = jax.ShapeDtypeStruct((2, WIDTH, N), jnp.float32)
FIELD_BUFFER = pltpu.VMEM(FIELD.shape, jnp.float32)
SEMS = pltpu.SemaphoreType.DMA((TILES, 2, 2))
BUFFER = pltpu.VMEM(CHAIN, jnp.float32)
HELD = pltpu.VMEM((BLOCKS, 2, 3 * HALF, LANES), jnp.float32)


def call(kernel, out_shape, operands, name, scratch=(), scalars=0, out_spec=WHOLE):
    outs = jax.tree.leaves(out_shape)
    size = sum(4 * math.prod(x.shape) for x in outs) + sum(4 * x.size for x in operands)
    return pl.pallas_call(
        kernel,
        out_shape=out_shape,
        in_specs=[SCALAR] * scalars + [WHOLE] * (len(operands) - scalars),
        out_specs=jax.tree.map(lambda _: out_spec, out_shape),
        scratch_shapes=list(scratch),
        compiler_params=pltpu.CompilerParams(vmem_limit_bytes=VMEM_LIMIT),
        cost_estimate=pl.CostEstimate(flops=20 * size, bytes_accessed=size, transcendentals=0),
        name=name,
    )(*operands)


def exchange(packed):
    return lax.all_to_all(packed, "rows", split_axis=0, concat_axis=0, tiled=True)


def to_previous(value):
    count = lax.axis_size("depth")
    return lax.ppermute(value, "depth", [(s, (s - 1) % count) for s in range(count)])


def per_device(grad_arriving, loss_grad, t_entry, t_exit, fields_entry, fields_exit, led_index):
    first = (lax.axis_index("depth") == 0).astype(jnp.int32)
    info = jnp.stack([lax.axis_index("rows"), first]).astype(jnp.int32)
    all_x, all_y, turns = (jnp.asarray(table) for table in light_tables())
    both = call(
        enter_kernel,
        BOTH,
        [grad_arriving[0], jnp.where(first == 1, loss_grad, t_entry[0])],
        "enter",
        [BUFFER, BUFFER],
    )
    both, info = lax.optimization_barrier((both, info))
    wave, onward, lit_x, lit_y = call(
        column_kernel,
        (PACKED, PACKED, LIT_X, LIT_Y),
        [led_index, info, turns, all_x, all_y, exchange(both)],
        "columns",
        [BUFFER, HELD],
        2,
    )
    onward = to_previous(onward)
    wave = exchange(wave)
    grad_entry = call(
        entry_kernel,
        FIELD,
        [lit_x, lit_y, fields_entry[0], wave],
        "entry",
        [FIELD_BUFFER, SEMS],
        out_spec=OUTSIDE,
    )
    onward, grad_entry = lax.optimization_barrier((onward, grad_entry))
    grad_exit, leaving = call(
        exit_kernel,
        (FIELD, FIELD),
        [lit_x, lit_y, fields_exit[0], t_exit[0], exchange(onward)],
        "exit",
        [BUFFER, BUFFER, BUFFER, FIELD_BUFFER, FIELD_BUFFER, SEMS, SEMS],
        out_spec=OUTSIDE,
    )
    return (grad_entry[None], grad_exit[None], leaving[None])


def solution(mesh):
    spread = P("depth", None, "rows", None)
    return jax.shard_map(
        per_device,
        mesh=mesh,
        in_specs=(spread, P(None, "rows", None), spread, spread, spread, spread, P("depth", None)),
        out_specs=(spread, spread, spread),
        check_vma=False,
    )
```

```python
import functools
import math

import jax
import jax.numpy as jnp
import numpy as np
from jax import lax
from jax.experimental import pallas as pl
from jax.experimental.pallas import tpu as pltpu
from jax.sharding import PartitionSpec as P

LED_SIDE = 15
SPREAD = 3
BLOCKS = 32
N = 2048
WIDTH = N // BLOCKS
LANES = 2 * WIDTH
HALF = WIDTH // 2
TILES = HALF // 8
VMEM_LIMIT = 16 * 1024 * 1024

INVERSE = pow(SPREAD, -1, N)
_k = np.arange(N, dtype=np.int64)
GAUSS = np.exp(-2j * np.pi * ((SPREAD * _k * _k) % N) / N).sum() / N


def chirp_gain(distance):
    return complex(GAUSS * np.exp(2j * np.pi * ((INVERSE * distance * distance) % N) / N))


def shift_of(freq):
    pairs = SPREAD * (freq - BLOCKS // 2) % BLOCKS
    return 2 * pairs, chirp_gain(-pairs), chirp_gain(BLOCKS - pairs)


def plus(a, b):
    return (a[0] + b[0], a[1] + b[1])


def minus(a, b):
    return (a[0] - b[0], a[1] - b[1])


def times_i(a):
    return (-a[1], a[0])


def times(a, real, imag):
    return (a[0] * real - a[1] * imag, a[0] * imag + a[1] * real)


def scaled(a, factor):
    return times(a, np.float32(factor.real), np.float32(factor.imag))


def turned(a, step, count, sign):
    step = step * sign % count
    if step == 0:
        return a
    if 2 * step == count:
        return (-a[0], -a[1])
    if 4 * step == count:
        return times_i(a)
    if 4 * step == 3 * count:
        return (a[1], -a[0])
    if 8 * step % count == 0:
        root = np.float32(math.sqrt(0.5))
        eighth = 8 * step // count
        added, taken = (a[0] + a[1]) * root, (a[0] - a[1]) * root
        return {
            1: (taken, added),
            3: (-added, taken),
            5: (-taken, -added),
            7: (added, -taken),
        }[eighth]
    angle = 2.0 * math.pi * step / count
    return scaled(a, complex(math.cos(angle), math.sin(angle)))


def small_dft(values, sign):
    count = len(values)
    if count == 1:
        return values
    if count == 2:
        return [plus(*values), minus(*values)]
    quarter = count // 4
    parts = [small_dft(values[phase::4], sign) for phase in range(4)]
    result = [None] * count
    for j in range(quarter):
        a, b, c, d = (turned(parts[k][j], j * k, count, sign) for k in range(4))
        sum_ac, dif_ac, sum_bd, dif_bd = plus(a, c), minus(a, c), plus(b, d), minus(b, d)
        result[j] = plus(sum_ac, sum_bd)
        result[j + 2 * quarter] = minus(sum_ac, sum_bd)
        up = (dif_ac[0] - dif_bd[1], dif_ac[1] + dif_bd[0])
        down = (dif_ac[0] + dif_bd[1], dif_ac[1] - dif_bd[0])
        result[j + quarter], result[j + 3 * quarter] = (up, down) if sign > 0 else (down, up)
    return result


def lane_ids():
    return lax.broadcasted_iota(jnp.int32, (8, LANES), 1)


def halves(first, second):
    low = lane_ids() < WIDTH
    return (
        jnp.where(low, first, pltpu.roll(second, WIDTH, 1)),
        jnp.where(low, pltpu.roll(first, WIDTH, 1), second),
    )


def tile(index):
    return pl.ds(8 * index, 8)


def get(ref, block, rows):
    return (ref[block, 0, rows, :], ref[block, 1, rows, :])


def put(ref, block, rows, value):
    ref[block, 0, rows, :] = value[0]
    ref[block, 1, rows, :] = value[1]


def block_dft(load, emit, stage, rows, sign):
    half = BLOCKS // 2
    for j, value in enumerate(small_dft([load(2 * n) for n in range(half)], sign)):
        put(stage, j, rows, value)
    odd = small_dft([load(2 * n + 1) for n in range(half)], sign)
    for j, value in enumerate(odd):
        even, value = get(stage, j, rows), turned(value, j, BLOCKS, sign)
        emit(j, plus(even, value))
        emit(j + half, minus(even, value))


def along_lanes(index, source, target, stage, moved):
    inside = lane_ids() % WIDTH
    rows = tile(index)

    def move(freq, value):
        shift, plain, wrapped = shift_of(freq)
        if shift:
            mask = inside >= shift
            value = tuple(
                jnp.where(mask, pltpu.roll(v, shift, 1), pltpu.roll(v, shift + WIDTH, 1))
                for v in value
            )
            real = jnp.where(mask, np.float32(plain.real), np.float32(wrapped.real))
            imag = jnp.where(mask, np.float32(plain.imag), np.float32(wrapped.imag))
            value = times(value, real, imag)
        else:
            value = scaled(value, plain)
        put(moved, freq, rows, value)

    block_dft(lambda block: get(source, block, rows), move, stage, rows, -1)
    block_dft(
        lambda freq: get(moved, freq, rows),
        lambda block, value: put(target, block, rows, value),
        stage,
        rows,
        1,
    )


def along_rows(load, store, stage, held):
    row_ids = lax.broadcasted_iota(jnp.int32, (8, LANES), 0)
    low = lane_ids() < WIDTH
    for index in range(TILES):
        rows = tile(index)

        def hold(freq, value):
            shift = shift_of(freq)[0]
            if shift > HALF:
                put(held, freq, rows, value)
            if shift:
                crossed = tuple(pltpu.roll(v, WIDTH, 1) for v in value)
                put(held, freq, pl.ds(HALF + 8 * index, 8), crossed)
            if shift < HALF:
                put(held, freq, pl.ds(2 * HALF + 8 * index, 8), value)

        block_dft(functools.partial(load, index), hold, stage, rows, -1)

    def shifted(index, freq):
        shift, plain, wrapped = shift_of(freq)
        begin = 2 * HALF - shift + 8 * index
        value = get(held, freq, pl.ds(begin, 8))
        if begin >= 2 * HALF:
            return scaled(value, plain)
        if begin + 8 <= HALF:
            return scaled(value, wrapped)
        mask = row_ids >= jnp.where(low, 2 * HALF - begin, HALF - begin)
        return times(
            value,
            jnp.where(mask, np.float32(plain.real), np.float32(wrapped.real)),
            jnp.where(mask, np.float32(plain.imag), np.float32(wrapped.imag)),
        )

    for index in range(TILES):
        block_dft(
            functools.partial(shifted, index),
            functools.partial(store, index),
            stage,
            tile(index),
            1,
        )


def natural(index, half):
    return pl.ds(8 * index + HALF * half, 8)


def field_copies(source, target, sems):
    return [
        [
            pltpu.make_async_copy(
                source.at[part, natural(index, half), :],
                target.at[part, natural(index, half), :],
                sems.at[index, part, half],
            )
            for part in range(2)
            for half in range(2)
        ]
        for index in range(TILES)
    ]


def start(copies):
    for tile_copies in copies:
        for copy in tile_copies:
            copy.start()


def wait(tile_copies):
    for copy in tile_copies:
        copy.wait()


def read_field(ref, index, write):
    for pair in range(BLOCKS // 2):
        cols = pl.ds(pair * LANES, LANES)
        parts = [
            halves(ref[part, natural(index, 0), cols], ref[part, natural(index, 1), cols])
            for part in range(2)
        ]
        for side in range(2):
            write(2 * pair + side, (parts[0][side], parts[1][side]))


def enter_kernel(field_ref, other_ref, out_ref, stage, moved):
    grad_out, other_out = out_ref.at[:, 0], out_ref.at[:, 1]
    for index in range(TILES):
        read_field(
            field_ref, index, lambda block, value: put(grad_out, block, tile(index), value)
        )
        along_lanes(index, grad_out, grad_out, stage, moved)
    for index in range(TILES):
        read_field(
            other_ref, index, lambda block, value: put(other_out, block, tile(index), value)
        )


def column_kernel(
    led_ref,
    info_ref,
    turn_ref,
    all_x_ref,
    all_y_ref,
    in_ref,
    wave_ref,
    out_ref,
    lit_x_ref,
    lit_y_ref,
    stage,
    held,
):
    use_loss = info_ref[1] == 1
    along_rows(
        lambda index, block: get(in_ref.at[:, 0], block, tile(index)),
        lambda index, block, value: put(wave_ref, block, tile(index), value),
        stage,
        held,
    )

    def passing(index, block):
        real, imag = get(wave_ref, block, tile(index))
        t_real, t_imag = get(in_ref.at[:, 1], block, tile(index))
        return (
            jnp.where(use_loss, t_real, real * t_real + imag * t_imag),
            jnp.where(use_loss, t_imag, imag * t_real - real * t_imag),
        )

    along_rows(
        passing,
        lambda index, block, value: put(out_ref, block, tile(index), value),
        stage,
        held,
    )
    for tick in range(2):
        write_light(tick, led_ref, info_ref, turn_ref, all_x_ref, all_y_ref, lit_x_ref, lit_y_ref)


def light_tables():
    shifts = np.arange(LED_SIDE) - LED_SIDE // 2
    along_x = np.exp(2j * np.pi * (shifts[:, None] * np.arange(N) % N) / N)
    along_y = np.zeros((WIDTH, LANES), np.complex128)
    along_y[:, :LED_SIDE] = np.exp(2j * np.pi * (np.arange(WIDTH)[:, None] * shifts % N) / N)
    turns = np.exp(2j * np.pi * np.arange(BLOCKS) / BLOCKS)
    return (
        np.concatenate([along_x.real, along_x.imag]).reshape(-1, N // LANES, LANES).astype(np.float32),
        np.stack([along_y.real, along_y.imag]).astype(np.float32),
        np.stack([np.tile(part[:, None], LANES) for part in (turns.real, turns.imag)]).astype(
            np.float32
        ),
    )


def write_light(
    tick, led_ref, info_ref, turn_ref, all_x_ref, all_y_ref, lit_x_ref, lit_y_ref
):
    led = led_ref[0, tick]
    column_shift = led // LED_SIDE
    row_shift = led - column_shift * LED_SIDE
    turn = (info_ref[0] * (row_shift - LED_SIDE // 2)) & (BLOCKS - 1)
    turns = [turn_ref[part, pl.ds(turn, 1), :] for part in range(2)]
    chosen = lane_ids() == row_shift
    for part in range(2):
        lit_x_ref[tick, part] = all_x_ref[column_shift + part * LED_SIDE]
    for index in range(WIDTH // 8):
        rows = tile(index)
        pair = tuple(
            jnp.sum(jnp.where(chosen, all_y_ref[part, rows, :], 0.0), axis=1, keepdims=True)
            for part in range(2)
        )
        pair = times(tuple(jnp.broadcast_to(v, (8, LANES)) for v in pair), *turns)
        for part in range(2):
            lit_y_ref[tick, part, rows, :] = pair[part]


def write_products(tick, index, wave_ref, lit_x_ref, lit_y_ref, field_ref, out_ref, *plain):
    lit_y = [
        [lit_y_ref[tick, part, natural(index, half), :] for part in range(2)]
        for half in range(2)
    ]
    for pair in range(BLOCKS // 2):
        cols = pl.ds(pair * LANES, LANES)
        left = get(wave_ref, 2 * pair, tile(index))
        right = get(wave_ref, 2 * pair + 1, tile(index))
        reals, imags = halves(left[0], right[0]), halves(left[1], right[1])
        lit_x = [lit_x_ref[tick, part, pair : pair + 1, :] for part in range(2)]
        for half in range(2):
            rows = natural(index, half)
            real, imag = reals[half], imags[half]
            if plain:
                t_ref, plain_ref = plain
                t_real, t_imag = t_ref[0, rows, cols], t_ref[1, rows, cols]
                plain_ref[0, rows, cols] = real * t_real + imag * t_imag
                plain_ref[1, rows, cols] = imag * t_real - real * t_imag
            lit = times(lit_y[half], *lit_x)
            f_real, f_imag = times(lit, field_ref[0, rows, cols], field_ref[1, rows, cols])
            out_ref[0, rows, cols] = real * f_real + imag * f_imag
            out_ref[1, rows, cols] = imag * f_real - real * f_imag


def entry_kernel(lit_x_ref, lit_y_ref, field_ref, wave_ref, out_hbm, out, sems):
    outs = field_copies(out, out_hbm, sems)
    for index in range(TILES):
        write_products(0, index, wave_ref, lit_x_ref, lit_y_ref, field_ref, out)
        start([outs[index]])
    for index in range(TILES):
        wait(outs[index])


def exit_kernel(
    lit_x_ref,
    lit_y_ref,
    field_ref,
    t_ref,
    in_ref,
    out_hbm,
    plain_hbm,
    packed,
    stage,
    moved,
    out,
    plain,
    out_sems,
    plain_sems,
):
    outs = field_copies(out, out_hbm, out_sems)
    plains = field_copies(plain, plain_hbm, plain_sems)
    for index in range(TILES):
        along_lanes(index, in_ref, packed, stage, moved)
        write_products(1, index, packed, lit_x_ref, lit_y_ref, field_ref, out, t_ref, plain)
        start([outs[index], plains[index]])
    for index in range(TILES):
        wait(outs[index] + plains[index])


WHOLE = pl.BlockSpec(memory_space=pltpu.VMEM)
SCALAR = pl.BlockSpec(memory_space=pltpu.SMEM)
OUTSIDE = pl.BlockSpec(memory_space=pltpu.HBM)
CHAIN = (BLOCKS, 2, HALF, LANES)
PACKED = jax.ShapeDtypeStruct(CHAIN, jnp.float32)
LIT_X = jax.ShapeDtypeStruct((2, 2, N // LANES, LANES), jnp.float32)
LIT_Y = jax.ShapeDtypeStruct((2, 2, WIDTH, LANES), jnp.float32)
BOTH = jax.ShapeDtypeStruct((BLOCKS, 2, 2, HALF, LANES), jnp.float32)
FIELD = jax.ShapeDtypeStruct((2, WIDTH, N), jnp.float32)
FIELD_BUFFER = pltpu.VMEM(FIELD.shape, jnp.float32)
SEMS = pltpu.SemaphoreType.DMA((TILES, 2, 2))
BUFFER = pltpu.VMEM(CHAIN, jnp.float32)
HELD = pltpu.VMEM((BLOCKS, 2, 3 * HALF, LANES), jnp.float32)


def call(kernel, out_shape, operands, name, scratch=(), scalars=0, out_spec=WHOLE):
    outs = jax.tree.leaves(out_shape)
    size = sum(4 * math.prod(x.shape) for x in outs) + sum(4 * x.size for x in operands)
    return pl.pallas_call(
        kernel,
        out_shape=out_shape,
        in_specs=[SCALAR] * scalars + [WHOLE] * (len(operands) - scalars),
        out_specs=jax.tree.map(lambda _: out_spec, out_shape),
        scratch_shapes=list(scratch),
        compiler_params=pltpu.CompilerParams(vmem_limit_bytes=VMEM_LIMIT),
        cost_estimate=pl.CostEstimate(flops=20 * size, bytes_accessed=size, transcendentals=0),
        name=name,
    )(*operands)


def exchange(packed):
    return lax.all_to_all(packed, "rows", split_axis=0, concat_axis=0, tiled=True)


def to_previous(value):
    count = lax.axis_size("depth")
    return lax.ppermute(value, "depth", [(s, (s - 1) % count) for s in range(count)])


def per_device(grad_arriving, loss_grad, t_entry, t_exit, fields_entry, fields_exit, led_index):
    first = (lax.axis_index("depth") == 0).astype(jnp.int32)
    info = jnp.stack([lax.axis_index("rows"), first]).astype(jnp.int32)
    all_x, all_y, turns = (jnp.asarray(table) for table in light_tables())
    both = call(
        enter_kernel,
        BOTH,
        [grad_arriving[0], jnp.where(first == 1, loss_grad, t_entry[0])],
        "enter",
        [BUFFER, BUFFER],
    )
    both, info = lax.optimization_barrier((both, info))
    wave, onward, lit_x, lit_y = call(
        column_kernel,
        (PACKED, PACKED, LIT_X, LIT_Y),
        [led_index, info, turns, all_x, all_y, exchange(both)],
        "columns",
        [BUFFER, HELD],
        2,
    )
    onward = to_previous(onward)
    wave = exchange(wave)
    grad_entry = call(
        entry_kernel,
        FIELD,
        [lit_x, lit_y, fields_entry[0], wave],
        "entry",
        [FIELD_BUFFER, SEMS],
        out_spec=OUTSIDE,
    )
    onward, grad_entry = lax.optimization_barrier((onward, grad_entry))
    grad_exit, leaving = call(
        exit_kernel,
        (FIELD, FIELD),
        [lit_x, lit_y, fields_exit[0], t_exit[0], exchange(onward)],
        "exit",
        [BUFFER, BUFFER, BUFFER, FIELD_BUFFER, FIELD_BUFFER, SEMS, SEMS],
        out_spec=OUTSIDE,
    )
    return (grad_entry[None], grad_exit[None], leaving[None])


def solution(mesh):
    spread = P("depth", None, "rows", None)
    return jax.shard_map(
        per_device,
        mesh=mesh,
        in_specs=(spread, P(None, "rows", None), spread, spread, spread, spread, P("depth", None)),
        out_specs=(spread, spread, spread),
        check_vma=False,
    )
```
